512 devices in a mesh: dp: 16 (over z), seq: 4 (over y_hi, core), tensor: 8 (over y_lo, x).
Axes of the slice: x: 4, y: 4 (y_hi: 2, y_lo: 2; y = y_hi * 2 + y_lo), z: 16, core: 2. Of those that a mesh axis runs over, the one named last changes fastest.
Arguments:
- student_hidden: bfloat16 [4, 64, 16, 4096], P('seq', None, None, 'tensor'), may hold values from -1.5 to 1.5
- teacher_hidden: bfloat16 [4, 64, 16, 16384], P('seq', None, 'dp', 'tensor'), may hold values from -24 to 24
- proj_weight: bfloat16 [4096, 16384], P('tensor', 'dp'), may hold values from -0.375 to 0.375
Outputs:
- loss_value: float32 [], replicated
- grad_weight: float32 [4096, 16384], P('tensor', 'dp')
- grad_input: bfloat16 [4, 64, 16, 4096], P('seq', 'dp', None, 'tensor')
The draws below stay inside these ranges and needn't reach their ends.
All inputs are finite; a program needn't handle non-finite values.
Results may differ from the reference program's by a relative error of at most 0.0028.
The reference program's roundings to bfloat16 on the way (of `quantized` and `grad_out`) count: a program that leaves them out, or rounds other values in their place, can miss the bound.
Values may be sent and summed in bfloat16 or wider, within the bound.
No kernel may reach another device: no remote copies, remote signals or barrier semaphores. Data moves between devices by JAX's collectives and lax.ppermute only.
A program may use at most 128 MiB of HBM per device.

```python
import math
import jax
import jax.numpy as jnp

D = 4096
DT = 16384
BLOCKS = 4
RA = 64
RB = 16


def draw_teacher_hidden(key, part):
    key = jax.random.fold_in(key, 7)
    key_base, key_rows = jax.random.split(key, 2)
    shape = (BLOCKS, RA, RB, DT)
    row_scale = jnp.exp(jax.random.uniform(key_rows, (BLOCKS, RA, RB, 1), jnp.float32, math.log(0.25), math.log(4.0)))
    base = jnp.clip(jax.random.normal(key_base, shape, jnp.float32), -6.0, 6.0)
    values = base * row_scale
    return values.astype(jnp.bfloat16)


def steps_of(own_key, dims, cuts, low, top_value):
    gain = 1.0
    for axis_at, parts in cuts:
        steps = jax.random.uniform(jax.random.fold_in(jax.random.fold_in(own_key, 6), axis_at), (parts,), jnp.float32, low / len(cuts), top_value / len(cuts))
        gain = gain * jnp.repeat(jnp.exp(steps), dims[axis_at] // parts).reshape((-1,) + (1,) * (len(dims) - 1 - axis_at))
    return gain


def centred(key, extent, scale, most, shards=(), held_as=jnp.bfloat16):
    array = scale * jax.random.normal(key, extent, jnp.float32)
    if shards:
        array = array * steps_of(key, extent, shards, -0.22, 0.18)
    return jnp.clip(array, -most, most).astype(held_as)


def setup_inputs(seed: int = 0) -> dict:
    keys = jax.random.split(jax.random.key(seed), 4)
    return {
        "student_hidden": centred(keys[0], (BLOCKS, RA, RB, D), 0.25, 1.5, ((0, 4), (3, 8))),
        "teacher_hidden": draw_teacher_hidden(jax.random.fold_in(keys[3], 71), 0),
        "proj_weight": centred(keys[2], (D, DT), (D // 16) ** -0.5, 0.375, ((0, 8), (1, 16))),
    }


scale_epsilon = 1e-6
grad_factor = 0.25


def reference(student_hidden, teacher_hidden, proj_weight):
    flat_rows = student_hidden.reshape(-1, D)
    teacher_rows = teacher_hidden.reshape(-1, DT).astype(jnp.float32)
    largest = jnp.max(jnp.abs(teacher_rows), axis=1, keepdims=True)
    token_scale = largest + scale_epsilon
    quantized = (teacher_rows / token_scale).astype(jnp.bfloat16)
    prediction = jnp.dot(flat_rows, proj_weight, preferred_element_type=jnp.float32)
    difference = prediction / token_scale - quantized.astype(jnp.float32)
    token_total = flat_rows.shape[0]
    loss_value = jnp.sum(difference * difference) / (token_total * DT)
    grad_out = ((difference / token_scale) * grad_factor).astype(jnp.bfloat16)
    grad_weight = jnp.dot(flat_rows.T, grad_out, preferred_element_type=jnp.float32)
    grad_input = jnp.dot(grad_out, proj_weight.T, preferred_element_type=jnp.float32).astype(jnp.bfloat16)
    return loss_value, grad_weight, grad_input.reshape(student_hidden.shape)
```

```python
import jax
import jax.numpy as jnp
from jax import lax
from jax.experimental import pallas as pl
from jax.experimental.pallas import tpu as pltpu
from jax.sharding import PartitionSpec as P

scale_epsilon = 1e-06
grad_factor = 0.25
LANES = 128
META = 16
TOP = 14.0
bf16, f16, f32 = jnp.bfloat16, jnp.float16, jnp.float32


def call(kernel, out_shape, flops, nbytes, **kw):
    return pl.pallas_call(
        kernel,
        out_shape=out_shape,
        cost_estimate=pl.CostEstimate(flops=flops, bytes_accessed=nbytes, transcendentals=0),
        compiler_params=pltpu.CompilerParams(vmem_limit_bytes=40 * 1024 * 1024),
        **kw,
    )


def all_to_all(x, axis):
    return lax.all_to_all(x, axis, 0, 0)


def exponent_of(largest):
    return jnp.clip(jnp.ceil(jnp.log2(jnp.maximum(largest, 1e-30))), -100.0, 100.0)


def pack_teacher(x_ref, o_ref):
    rows = x_ref[...].astype(f32)
    largest = jnp.max(jnp.max(jnp.abs(rows).reshape(8, 8, -1), axis=0), axis=1, keepdims=True)
    half = rows.shape[1] // 2
    wide = jnp.broadcast_to(jnp.concatenate([largest, largest], axis=0), (16, LANES)).astype(bf16)
    for t in range(8):
        block = rows[8 * t : 8 * t + 8]
        both = jnp.concatenate([block[:, :half], block[:, half:]], axis=0)
        o_ref[16 * t : 16 * t + 16, :half] = both.astype(bf16)
        o_ref[16 * t : 16 * t + 16, half:] = wide


def forward(s_ref, w_ref, o_ref):
    partial = jnp.dot(s_ref[...], w_ref[...], preferred_element_type=f32)
    power = exponent_of(jnp.max(jnp.abs(partial), axis=1, keepdims=True))
    scaled = partial * jnp.exp2(TOP - power)
    rows, width = scaled.shape
    for c in range(width // LANES):
        o_ref[0, c * rows : (c + 1) * rows, :] = scaled[:, c * LANES : (c + 1) * LANES]
    meta = jnp.transpose(jnp.broadcast_to(power, (rows, LANES)))
    o_ref[0, width // LANES * rows :, :] = meta[:META]


def token_grad(pred_ref, tgt_ref, o_ref, held):
    blocks, rows, _ = pred_ref.shape

    @pl.when(pl.program_id(0) == 0)
    def _():
        r = lax.broadcasted_iota(jnp.int32, (rows, rows), 0)
        q = lax.broadcasted_iota(jnp.int32, (rows, rows), 1)
        order = jnp.where(q == (r % 16) * 8 + r // 16, 1.0, 0.0).astype(bf16)
        target = jnp.dot(order, tgt_ref[...], preferred_element_type=f32)
        token_scale = target[:, blocks * LANES : blocks * LANES + 1] + scale_epsilon
        total = jnp.zeros((rows, LANES), f32)
        for c in range(blocks):
            quantized = (target[:, c * LANES : (c + 1) * LANES] / token_scale).astype(bf16)
            difference = pred_ref[c] / token_scale - quantized.astype(f32)
            total = total + difference * difference
            held[c * rows : (c + 1) * rows, :] = ((difference / token_scale) * grad_factor).astype(bf16)
        loss = jnp.sum(jnp.sum(total, axis=0, keepdims=True), axis=1, keepdims=True)
        high = loss.astype(bf16).astype(f32)
        middle = (loss - high).astype(bf16).astype(f32)
        low = loss - high - middle
        row = lax.broadcasted_iota(jnp.int32, (META, LANES), 0)
        pieces = jnp.where(row == 0, high, jnp.where(row == 1, middle, jnp.where(row == 2, low, 0.0)))
        held[blocks * rows :, :] = pieces.astype(bf16)

    o_ref[0] = held[...]


def input_grad(g_ref, w_ref, o_ref, loss_ref):
    rows = 128

    @pl.when(pl.program_id(0) == 0)
    def _():
        loss_ref[...] = jnp.zeros_like(loss_ref)

    pieces = g_ref[0, 8 * rows :, :].astype(f32)
    loss_ref[...] += jnp.sum(pieces, axis=0, keepdims=True)
    grad = jnp.concatenate([g_ref[0, c * rows : (c + 1) * rows, :] for c in range(8)], axis=1)
    partial = lax.dot_general(grad, w_ref[...], (((1,), (1,)), ((), ())), preferred_element_type=f32)
    for n in range(2):
        chunk = partial[64 * n : 64 * n + 64]
        largest = jnp.max(jnp.max(jnp.abs(chunk), axis=0, keepdims=True), axis=1, keepdims=True)
        power = exponent_of(largest)
        scaled = chunk * jnp.exp2(TOP - power)
        for c in range(4):
            o_ref[n, 64 * c : 64 * c + 64, :] = scaled[:, c * LANES : (c + 1) * LANES]
        o_ref[n, 256:, :] = jnp.broadcast_to(power, (META, LANES))


def weight_grad(core_ref, s_ref, g_ref, after_ref, send_ref, keep_ref):
    del after_ref
    tokens, width = s_ref.shape
    half = width // 2
    rows = 128
    grad = jnp.concatenate(
        [g_ref[:, c * rows : (c + 1) * rows, :].reshape(tokens, LANES) for c in range(2)], axis=1
    )
    core = core_ref[0]
    for ref, which in ((send_ref, 1 - core), (keep_ref, core)):
        part = s_ref[:, pl.ds(pl.multiple_of(which * half, half), half)]
        ref[...] = lax.dot_general(part, grad, (((0,), (0,)), ((), ())), preferred_element_type=f32)


def body(student_hidden, teacher_hidden, proj_weight):
    width_local = student_hidden.shape[3]
    student = student_hidden.reshape(-1, width_local)
    tokens, columns = student.shape[0], proj_weight.shape[1]
    tensor_count, dp_count, seq_count = (lax.axis_size(a) for a in ("tensor", "dp", "seq"))
    own = tokens // tensor_count
    blocks = columns // LANES

    with jax.named_scope("teacher"):
        spread = all_to_all(teacher_hidden.reshape(8, 8, -1), "tensor")
        packed = call(
            pack_teacher,
            jax.ShapeDtypeStruct((128, columns + LANES), bf16),
            0,
            600_000,
        )(spread.reshape(64, -1))
        target = all_to_all(packed.reshape(16, 8, -1), "dp").reshape(own, -1)

    with jax.named_scope("prediction"):
        size = blocks * own + META
        partial = call(
            forward,
            jax.ShapeDtypeStruct((tensor_count, size, LANES), f32),
            2 * tokens * width_local * columns,
            6_000_000,
            grid=(tensor_count,),
            in_specs=[
                pl.BlockSpec((own, width_local), lambda i: (i, 0)),
                pl.BlockSpec((width_local, columns), lambda i: (0, 0)),
            ],
            out_specs=pl.BlockSpec((1, size, LANES), lambda i: (i, 0, 0)),
        )(student, proj_weight)
        parts = all_to_all(partial.astype(f16), "tensor").astype(f32)
        unscale = jnp.exp2(parts[:, blocks * own, :] - TOP)
        data = parts[:, : blocks * own, :].reshape(tensor_count, blocks, own, LANES)
        prediction = jnp.sum(data * unscale[:, None, :, None], axis=0)

    with jax.named_scope("gradient"):
        grad_own = call(
            token_grad,
            jax.ShapeDtypeStruct((tensor_count, size, LANES), bf16),
            2 * own * own * columns,
            3_000_000,
            grid=(tensor_count,),
            in_specs=[
                pl.BlockSpec((blocks, own, LANES), lambda i: (0, 0, 0)),
                pl.BlockSpec((own, columns + LANES), lambda i: (0, 0)),
            ],
            out_specs=pl.BlockSpec((1, size, LANES), lambda i: (i, 0, 0)),
            scratch_shapes=[pltpu.VMEM((size, LANES), bf16)],
        )(prediction, target)
        grad = all_to_all(grad_own, "tensor")

    with jax.named_scope("input_grad"):
        chunk = 64 * 4 + META
        term, loss = call(
            input_grad,
            (jax.ShapeDtypeStruct((dp_count, chunk, LANES), f32), jax.ShapeDtypeStruct((1, LANES), f32)),
            2 * tokens * width_local * columns,
            5_000_000,
            grid=(tensor_count,),
            in_specs=[
                pl.BlockSpec((1, size, LANES), lambda i: (i, 0, 0)),
                pl.BlockSpec((width_local, columns), lambda i: (0, 0)),
            ],
            out_specs=(
                pl.BlockSpec((2, chunk, LANES), lambda i: (i, 0, 0)),
                pl.BlockSpec((1, LANES), lambda i: (0, 0)),
            ),
        )(grad, proj_weight)
        terms = all_to_all(term.astype(f16), "dp").astype(f32)
        unscale = jnp.exp2(terms[:, 256:257, 0:1] - TOP)
        summed = jnp.sum(terms[:, :256, :] * unscale, axis=0)
        grad_input = jnp.transpose(summed.reshape(4, 64, LANES), (1, 0, 2)).astype(bf16)
        grad_input = grad_input.reshape(1, 4, 16, width_local)

    with jax.named_scope("weight_grad"):
        seq_index = lax.axis_index("seq")
        core = seq_index % 2
        other_core = [(i, i ^ 1) for i in range(seq_count)]
        other_y = [(i, i ^ 2) for i in range(seq_count)]
        half = jax.ShapeDtypeStruct((width_local // 2, columns), f32)
        send, keep = call(
            weight_grad,
            (half, half),
            2 * tokens * width_local * columns,
            5_000_000,
            grid=(4,),
            in_specs=[
                pl.BlockSpec(memory_space=pltpu.SMEM),
                pl.BlockSpec((tokens, width_local), lambda i: (0, 0)),
                pl.BlockSpec((tensor_count, 2 * own, LANES), lambda i: (0, i, 0)),
                pl.BlockSpec((1, LANES), lambda i: (0, 0)),
            ],
            out_specs=(
                pl.BlockSpec((width_local // 2, 2 * LANES), lambda i: (0, i)),
                pl.BlockSpec((width_local // 2, 2 * LANES), lambda i: (0, i)),
            ),
        )(core.reshape(1).astype(jnp.int32), student, grad, loss)
        pair = (keep + lax.ppermute(send, "seq", other_core)).astype(bf16)
        mine = pair.astype(f32) + lax.ppermute(pair, "seq", other_y).astype(f32)
        theirs = lax.ppermute(mine, "seq", other_core)
        grad_weight = jnp.where(
            core == 0,
            jnp.concatenate([mine, theirs], axis=0),
            jnp.concatenate([theirs, mine], axis=0),
        )

    with jax.named_scope("loss"):
        for axis, step in (("dp", 1), ("dp", 2), ("dp", 4), ("dp", 8), ("seq", 1), ("seq", 2)):
            moves = [(i, i ^ step) for i in range(lax.axis_size(axis))]
            loss = loss + lax.ppermute(loss, axis, moves)
        loss_value = loss[0, 0] / (tokens * seq_count * columns * dp_count)
    return (loss_value, grad_weight, grad_input)


def solution(mesh):
    placed = (P("seq", None, None, "tensor"), P("seq", None, "dp", "tensor"), P("tensor", "dp"))
    return jax.shard_map(
        body,
        mesh=mesh,
        in_specs=placed,
        out_specs=(P(), P("tensor", "dp"), P("seq", "dp", None, "tensor")),
        check_vma=False,
    )
```

```python
import jax
import jax.numpy as jnp
from jax import lax
from jax.experimental import pallas as pl
from jax.experimental.pallas import tpu as pltpu
from jax.sharding import PartitionSpec as P

scale_epsilon = 1e-06
grad_factor = 0.25
LANES = 128
META = 16
TOP = 14.0
bf16, f16, f32 = jnp.bfloat16, jnp.float16, jnp.float32


def call(kernel, out_shape, flops, nbytes, **kw):
    return pl.pallas_call(
        kernel,
        out_shape=out_shape,
        cost_estimate=pl.CostEstimate(flops=flops, bytes_accessed=nbytes, transcendentals=0),
        compiler_params=pltpu.CompilerParams(vmem_limit_bytes=16 * 1024 * 1024),
        **kw,
    )


def all_to_all(x, axis):
    return lax.all_to_all(x, axis, 0, 0)


def exponent_of(largest):
    return jnp.clip(jnp.ceil(jnp.log2(jnp.maximum(largest, 1e-30))), -100.0, 100.0)


def pack_teacher(place_ref, x_ref, *refs):
    held = refs[4]
    rows = x_ref[...].astype(f32)
    largest = jnp.max(jnp.max(jnp.abs(rows).reshape(8, 8, -1), axis=0), axis=1, keepdims=True)
    wide = jnp.broadcast_to(jnp.concatenate([largest, largest], axis=0), (16, LANES)).astype(bf16)
    half = rows.shape[1] // 4
    for t in range(8):
        for j in range(2):
            block = rows[8 * t : 8 * t + 8, 2 * half * j : 2 * half * (j + 1)]
            both = jnp.concatenate([block[:, :half], block[:, half:]], axis=0)
            low, high = 2 * (t % 2) + j, t // 2
            held[low, 16 * high : 16 * high + 16, :half] = both.astype(bf16)
            held[low, 16 * high : 16 * high + 16, half:] = wide
    for k in range(4):
        refs[k][...] = held[(place_ref[1] + k) & 3]


def regroup_teacher(place_ref, *refs):
    for m in range(4):
        high = (place_ref[0] + m) & 3
        for k in range(4):
            refs[4 + m][16 * k : 16 * k + 16, :] = refs[k][pl.ds(pl.multiple_of(16 * high, 16), 16), :]


def forward(s_ref, w_ref, o_ref):
    partial = jnp.dot(s_ref[...], w_ref[...], preferred_element_type=f32)
    power = exponent_of(jnp.max(jnp.abs(partial), axis=1, keepdims=True))
    scaled = partial * jnp.exp2(TOP - power)
    rows, width = scaled.shape[0] // 2, scaled.shape[1]
    for n in range(2):
        for c in range(width // LANES):
            o_ref[n, c * rows : (c + 1) * rows, :] = scaled[n * rows : (n + 1) * rows, c * LANES : (c + 1) * LANES]
        meta = jnp.transpose(jnp.broadcast_to(power[n * rows : (n + 1) * rows], (rows, LANES)))
        o_ref[n, width // LANES * rows :, :] = meta[:META]


def token_grad(place_ref, pred_ref, t0_ref, t1_ref, t2_ref, t3_ref, o_ref, held):
    blocks, rows, _ = pred_ref.shape

    @pl.when(pl.program_id(0) == 0)
    def _():
        arrived = jnp.concatenate([t0_ref[...], t1_ref[...], t2_ref[...], t3_ref[...]], axis=0)
        count, half = arrived.shape[0], blocks // 2 * LANES
        r = lax.broadcasted_iota(jnp.int32, (rows, count), 0)
        q = lax.broadcasted_iota(jnp.int32, (rows, count), 1)
        second = ((place_ref[0] - q // 64) & 3) * 4 + ((place_ref[1] - q // 16 % 4) & 3)
        match = r == (q % 8) * 16 + second
        first = jnp.where(match & (q // 8 % 2 == 0), 1.0, 0.0).astype(bf16)
        other = jnp.where(match & (q // 8 % 2 == 1), 1.0, 0.0).astype(bf16)
        left = jnp.dot(first, arrived, preferred_element_type=f32)
        right = jnp.dot(other, arrived[:, :half], preferred_element_type=f32)
        target = jnp.concatenate([left[:, :half], right], axis=1)
        token_scale = left[:, half : half + 1] + scale_epsilon
        total = jnp.zeros((rows, LANES), f32)
        for c in range(blocks):
            quantized = (target[:, c * LANES : (c + 1) * LANES] / token_scale).astype(bf16)
            difference = pred_ref[c] / token_scale - quantized.astype(f32)
            total = total + difference * difference
            held[c * rows : (c + 1) * rows, :] = ((difference / token_scale) * grad_factor).astype(bf16)
        loss = jnp.sum(jnp.sum(total, axis=0, keepdims=True), axis=1, keepdims=True)
        high = loss.astype(bf16).astype(f32)
        middle = (loss - high).astype(bf16).astype(f32)
        low = loss - high - middle
        row = lax.broadcasted_iota(jnp.int32, (META, LANES), 0)
        pieces = jnp.where(row == 0, high, jnp.where(row == 1, middle, jnp.where(row == 2, low, 0.0)))
        held[blocks * rows :, :] = pieces.astype(bf16)

    o_ref[0] = held[...]


def input_grad(g_ref, w_ref, loss_ref, o_ref, total_ref):
    rows = 128
    pieces = jnp.sum(loss_ref[...].astype(f32), axis=0)
    loss = jnp.sum(pieces, axis=0, keepdims=True)
    total_ref[...] = loss
    row = lax.broadcasted_iota(jnp.int32, (META, LANES), 0)
    loss_power = exponent_of(loss)
    scaled_loss = loss * jnp.exp2(10.0 - loss_power)
    high = jnp.floor(scaled_loss)
    rest = (scaled_loss - high) * 2048.0
    middle = jnp.floor(rest)
    low = jnp.floor((rest - middle) * 2048.0)
    meta = jnp.where(row == 1, loss_power, jnp.where(row == 2, high, jnp.where(row == 3, middle, low)))
    grad = jnp.concatenate(
        [
            jnp.concatenate([g_ref[n, c * rows : (c + 1) * rows, :] for c in range(8)], axis=1)
            for n in range(2)
        ],
        axis=0,
    )
    partial = lax.dot_general(grad, w_ref[...], (((1,), (1,)), ((), ())), preferred_element_type=f32)
    for n in range(4):
        chunk = partial[64 * n : 64 * n + 64]
        largest = jnp.max(jnp.max(jnp.abs(chunk), axis=0, keepdims=True), axis=1, keepdims=True)
        power = exponent_of(largest)
        scaled = chunk * jnp.exp2(TOP - power)
        for c in range(4):
            o_ref[n, 64 * c : 64 * c + 64, :] = scaled[:, c * LANES : (c + 1) * LANES]
        o_ref[n, 256:, :] = jnp.where(row == 0, power, meta)


def weight_grad(core_ref, s_ref, g_ref, after_ref, send_ref, keep_ref):
    del after_ref
    tokens, width = s_ref.shape
    half = width // 2
    rows = 128
    grad = jnp.concatenate(
        [g_ref[:, c * rows : (c + 1) * rows, :].reshape(tokens, LANES) for c in range(2)], axis=1
    )
    core = core_ref[0]
    for ref, which in ((send_ref, 1 - core), (keep_ref, core)):
        part = s_ref[:, pl.ds(pl.multiple_of(which * half, half), half)]
        ref[...] = lax.dot_general(part, grad, (((0,), (0,)), ((), ())), preferred_element_type=f32)


def body(student_hidden, teacher_hidden, proj_weight):
    width_local = student_hidden.shape[3]
    student = student_hidden.reshape(-1, width_local)
    tokens, columns = student.shape[0], proj_weight.shape[1]
    tensor_count, dp_count, seq_count = (lax.axis_size(a) for a in ("tensor", "dp", "seq"))
    own = tokens // tensor_count
    blocks = columns // LANES

    dp_index = lax.axis_index("dp").astype(jnp.int32)
    place = jnp.stack([dp_index // 4, dp_index % 4])
    scalars = pl.BlockSpec(memory_space=pltpu.SMEM)
    whole = pl.BlockSpec(memory_space=pltpu.VMEM)

    with jax.named_scope("teacher"):
        spread = all_to_all(teacher_hidden.reshape(8, 8, -1), "tensor")
        group = (jax.ShapeDtypeStruct((64, columns // 2 + LANES), bf16),) * 4
        packed = call(
            pack_teacher,
            group,
            0,
            600_000,
            in_specs=[scalars, whole],
            out_specs=(whole,) * 4,
            scratch_shapes=[pltpu.VMEM((4, 64, columns // 2 + LANES), bf16)],
        )(place, spread.reshape(64, -1))
        near = [packed[0]]
        for k in range(1, 4):
            moves = [(z, z // 4 * 4 + (z + k) % 4) for z in range(dp_count)]
            near.append(lax.ppermute(packed[k], "dp", moves))
        packed = call(
            regroup_teacher,
            group,
            0,
            600_000,
            in_specs=[scalars] + [whole] * 4,
            out_specs=(whole,) * 4,
        )(place, *near)
        target = [packed[0]]
        for m in range(1, 4):
            moves = [(z, (z + 4 * m) % dp_count) for z in range(dp_count)]
            target.append(lax.ppermute(packed[m], "dp", moves))

    with jax.named_scope("prediction"):
        size = blocks * own + META
        partial = call(
            forward,
            jax.ShapeDtypeStruct((tensor_count, size, LANES), f32),
            2 * tokens * width_local * columns,
            6_000_000,
            grid=(tensor_count // 2,),
            in_specs=[
                pl.BlockSpec((2 * own, width_local), lambda i: (i, 0)),
                pl.BlockSpec((width_local, columns), lambda i: (0, 0)),
            ],
            out_specs=pl.BlockSpec((2, size, LANES), lambda i: (i, 0, 0)),
        )(student, proj_weight)
        parts = all_to_all(partial.astype(f16), "tensor").astype(f32)
        unscale = jnp.exp2(parts[:, blocks * own, :] - TOP)
        data = parts[:, : blocks * own, :].reshape(tensor_count, blocks, own, LANES)
        prediction = jnp.sum(data * unscale[:, None, :, None], axis=0)

    with jax.named_scope("gradient"):
        grad_own = call(
            token_grad,
            jax.ShapeDtypeStruct((tensor_count, size, LANES), bf16),
            2 * own * own * columns,
            3_000_000,
            grid=(tensor_count,),
            in_specs=[scalars, pl.BlockSpec((blocks, own, LANES), lambda i: (0, 0, 0))]
            + [pl.BlockSpec(group[0].shape, lambda i: (0, 0))] * 4,
            out_specs=pl.BlockSpec((1, size, LANES), lambda i: (i, 0, 0)),
            scratch_shapes=[pltpu.VMEM((size, LANES), bf16)],
        )(place, prediction, *target)
        grad = all_to_all(grad_own, "tensor")

    with jax.named_scope("input_grad"):
        chunk = 64 * 4 + META
        term, total = call(
            input_grad,
            (jax.ShapeDtypeStruct((dp_count, chunk, LANES), f32), jax.ShapeDtypeStruct((1, LANES), f32)),
            2 * tokens * width_local * columns,
            5_000_000,
            grid=(tensor_count // 2,),
            in_specs=[
                pl.BlockSpec((2, size, LANES), lambda i: (i, 0, 0)),
                pl.BlockSpec((width_local, columns), lambda i: (0, 0)),
                pl.BlockSpec((tensor_count, META, LANES), lambda i: (0, blocks * own // META, 0)),
            ],
            out_specs=(
                pl.BlockSpec((4, chunk, LANES), lambda i: (i, 0, 0)),
                pl.BlockSpec((1, LANES), lambda i: (0, 0)),
            ),
        )(grad, proj_weight, grad)
        terms = all_to_all(term.astype(f16), "dp").astype(f32)
        unscale = jnp.exp2(terms[:, 256:257, 0:1] - TOP)
        summed = jnp.sum(terms[:, :256, :] * unscale, axis=0)
        grad_input = jnp.transpose(summed.reshape(4, 64, LANES), (1, 0, 2)).astype(bf16)
        grad_input = grad_input.reshape(1, 4, 16, width_local)

    with jax.named_scope("weight_grad"):
        seq_index = lax.axis_index("seq")
        core = seq_index % 2
        other_core = [(i, i ^ 1) for i in range(seq_count)]
        other_y = [(i, i ^ 2) for i in range(seq_count)]
        half = jax.ShapeDtypeStruct((width_local // 2, columns), f32)
        send, keep = call(
            weight_grad,
            (half, half),
            2 * tokens * width_local * columns,
            5_000_000,
            grid=(4,),
            in_specs=[
                scalars,
                pl.BlockSpec((tokens, width_local), lambda i: (0, 0)),
                pl.BlockSpec((tensor_count, 2 * own, LANES), lambda i: (0, i, 0)),
                pl.BlockSpec((1, LANES), lambda i: (0, 0)),
            ],
            out_specs=(
                pl.BlockSpec((width_local // 2, 2 * LANES), lambda i: (0, i)),
                pl.BlockSpec((width_local // 2, 2 * LANES), lambda i: (0, i)),
            ),
        )(core.reshape(1).astype(jnp.int32), student, grad, total)
        pair = (keep + lax.ppermute(send, "seq", other_core)).astype(bf16)
        mine = pair.astype(f32) + lax.ppermute(pair, "seq", other_y).astype(f32)
        theirs = lax.ppermute(mine, "seq", other_core)
        grad_weight = jnp.where(
            core == 0,
            jnp.concatenate([mine, theirs], axis=0),
            jnp.concatenate([theirs, mine], axis=0),
        )

    with jax.named_scope("loss"):
        pieces = terms[:, 257:261, 0]
        losses = (pieces[:, 1] + (pieces[:, 2] + pieces[:, 3] / 2048.0) / 2048.0) * jnp.exp2(pieces[:, 0] - 10.0)
        loss_value = lax.psum(jnp.sum(losses), "seq") / (tokens * seq_count * columns * dp_count)
    return (loss_value, grad_weight, grad_input)


def solution(mesh):
    placed = (P("seq", None, None, "tensor"), P("seq", None, "dp", "tensor"), P("tensor", "dp"))
    return jax.shard_map(
        body,
        mesh=mesh,
        in_specs=placed,
        out_specs=(P(), P("tensor", "dp"), P("seq", "dp", None, "tensor")),
        check_vma=False,
    )
```

```python
import jax
import jax.numpy as jnp
from jax import lax
from jax.experimental import pallas as pl
from jax.experimental.pallas import tpu as pltpu
from jax.sharding import PartitionSpec as P

scale_epsilon = 1e-06
grad_factor = 0.25
LANES = 128
META = 8
PIECES = 16
TOP = 14.0
bf16, f16, f32 = jnp.bfloat16, jnp.float16, jnp.float32


def call(kernel, out_shape, flops, nbytes, **kw):
    return pl.pallas_call(
        kernel,
        out_shape=out_shape,
        cost_estimate=pl.CostEstimate(flops=flops, bytes_accessed=nbytes, transcendentals=0),
        compiler_params=pltpu.CompilerParams(vmem_limit_bytes=16 * 1024 * 1024),
        **kw,
    )


def all_to_all(x, axis):
    return lax.all_to_all(x, axis, 0, 0)


def butterfly(x, steps):
    for axis, step in steps:
        x = x + lax.ppermute(x, axis, [(i, i ^ step) for i in range(lax.axis_size(axis))])
    return x


def exponent_of(largest):
    return jnp.clip(jnp.ceil(jnp.log2(jnp.maximum(largest, 1e-30))), -100.0, 100.0)


def pack_teacher(place_ref, x_ref, *refs):
    held = refs[4]
    rows = x_ref[...].astype(f32)
    largest = jnp.max(jnp.max(jnp.abs(rows).reshape(8, 8, -1), axis=0), axis=1, keepdims=True)
    wide = jnp.broadcast_to(jnp.concatenate([largest, largest], axis=0), (16, LANES)).astype(bf16)
    half = rows.shape[1] // 4
    for t in range(8):
        for j in range(2):
            block = rows[8 * t : 8 * t + 8, 2 * half * j : 2 * half * (j + 1)]
            both = jnp.concatenate([block[:, :half], block[:, half:]], axis=0)
            low, high = 2 * (t % 2) + j, t // 2
            held[low, 16 * high : 16 * high + 16, :half] = both.astype(bf16)
            held[low, 16 * high : 16 * high + 16, half:] = wide
    for k in range(4):
        refs[k][...] = held[(place_ref[1] + k) & 3]


def regroup_teacher(place_ref, *refs):
    for m in range(4):
        high = (place_ref[0] + m) & 3
        for k in range(4):
            refs[4 + m][16 * k : 16 * k + 16, :] = refs[k][pl.ds(pl.multiple_of(16 * high, 16), 16), :]


def forward(s_ref, w_ref, o_ref):
    partial = jnp.dot(s_ref[...], w_ref[...], preferred_element_type=f32)
    power = exponent_of(jnp.max(jnp.abs(partial), axis=1, keepdims=True))
    scaled = partial * jnp.exp2(TOP - power)
    rows, width = scaled.shape[0] // 2, scaled.shape[1]
    for n in range(2):
        for c in range(width // LANES):
            o_ref[n, c * rows : (c + 1) * rows, :] = scaled[n * rows : (n + 1) * rows, c * LANES : (c + 1) * LANES]
        meta = jnp.transpose(jnp.broadcast_to(power[n * rows : (n + 1) * rows], (rows, LANES)))
        o_ref[n, width // LANES * rows :, :] = meta[:META]


def token_grad(place_ref, pred_ref, t0_ref, t1_ref, t2_ref, t3_ref, a_ref, b_ref, held):
    blocks, rows, _ = pred_ref.shape

    @pl.when(pl.program_id(0) == 0)
    def _():
        arrived = jnp.concatenate([t0_ref[...], t1_ref[...], t2_ref[...], t3_ref[...]], axis=0)
        count, half = arrived.shape[0], blocks // 2 * LANES
        r = lax.broadcasted_iota(jnp.int32, (rows, count), 0)
        q = lax.broadcasted_iota(jnp.int32, (rows, count), 1)
        shift = q // 16 % 4
        shift = jnp.where(shift == 3, -1, shift)
        second = (place_ref[0] * 4 + place_ref[1] - 4 * (q // 64) - shift) & 15
        match = r == (q % 8) * 16 + second
        first = jnp.where(match & (q // 8 % 2 == 0), 1.0, 0.0).astype(bf16)
        other = jnp.where(match & (q // 8 % 2 == 1), 1.0, 0.0).astype(bf16)
        left = jnp.dot(first, arrived, preferred_element_type=f32)
        right = jnp.dot(other, arrived[:, :half], preferred_element_type=f32)
        target = jnp.concatenate([left[:, :half], right], axis=1)
        token_scale = left[:, half : half + 1] + scale_epsilon
        total = jnp.zeros((rows, LANES), f32)
        for c in range(blocks):
            quantized = (target[:, c * LANES : (c + 1) * LANES] / token_scale).astype(bf16)
            difference = pred_ref[c] / token_scale - quantized.astype(f32)
            total = total + difference * difference
            held[c * rows : (c + 1) * rows, :] = ((difference / token_scale) * grad_factor).astype(bf16)
        loss = jnp.sum(jnp.sum(total, axis=0, keepdims=True), axis=1, keepdims=True)
        high = loss.astype(bf16).astype(f32)
        middle = (loss - high).astype(bf16).astype(f32)
        low = loss - high - middle
        row = lax.broadcasted_iota(jnp.int32, (PIECES, LANES), 0)
        pieces = jnp.where(row == 0, high, jnp.where(row == 1, middle, jnp.where(row == 2, low, 0.0)))
        held[blocks * rows :, :] = pieces.astype(bf16)

    part = rows // 2
    for ref, chunk in ((a_ref, 1 - place_ref[2]), (b_ref, place_ref[2])):
        for c in range(blocks):
            start = pl.multiple_of(c * rows + chunk * part, part)
            ref[0, c * part : (c + 1) * part, :] = held[pl.ds(start, part), :]
    a_ref[0, blocks * part :, :] = held[blocks * rows :, :]


def scaled_by_power(chunk):
    largest = jnp.max(jnp.max(jnp.abs(chunk), axis=0, keepdims=True), axis=1, keepdims=True)
    power = exponent_of(largest)
    return chunk * jnp.exp2(TOP - power), power


def loss_rows(loss):
    row = lax.broadcasted_iota(jnp.int32, (META, LANES), 0)
    power = exponent_of(loss)
    scaled = loss * jnp.exp2(10.0 - power)
    high = jnp.floor(scaled)
    rest = (scaled - high) * 2048.0
    middle = jnp.floor(rest)
    low = jnp.floor((rest - middle) * 2048.0)
    return row, jnp.where(row == 1, power, jnp.where(row == 2, high, jnp.where(row == 3, middle, low)))


def chunk_terms(g_ref, w_ref):
    part = 64
    grad = jnp.concatenate(
        [
            jnp.concatenate([g_ref[n, c * part : (c + 1) * part, :] for c in range(8)], axis=1)
            for n in range(g_ref.shape[0])
        ],
        axis=0,
    )
    terms = lax.dot_general(grad, w_ref[...], (((1,), (1,)), ((), ())), preferred_element_type=f32)
    return [terms[n * part : (n + 1) * part] for n in range(g_ref.shape[0])]


def send_terms(g_ref, w_ref, loss_ref, send_ref, total_ref):
    pieces = jnp.sum(loss_ref[...].astype(f32), axis=0)
    total_ref[...] = jnp.sum(pieces, axis=0, keepdims=True)
    for n, chunk in enumerate(chunk_terms(g_ref, w_ref)):
        scaled, power = scaled_by_power(chunk)
        for c in range(4):
            send_ref[n, 64 * c : 64 * c + 64, :] = scaled[:, c * LANES : (c + 1) * LANES]
        send_ref[n, 256:, :] = jnp.broadcast_to(power, (META, LANES))


def keep_terms(g_ref, w_ref, got_ref, loss_ref, o_ref):
    row, meta = loss_rows(loss_ref[...])
    for n, chunk in enumerate(chunk_terms(g_ref, w_ref)):
        got = jnp.concatenate([got_ref[n, 64 * c : 64 * c + 64, :] for c in range(4)], axis=1)
        chunk = chunk + got * jnp.exp2(got_ref[n, 256:257, 0:1] - TOP)
        scaled, power = scaled_by_power(chunk)
        for c in range(4):
            o_ref[n, 64 * c : 64 * c + 64, :] = scaled[:, c * LANES : (c + 1) * LANES]
        o_ref[n, 256:, :] = jnp.where(row == 0, power, meta)


def weight_grad(place_ref, s_ref, t_ref, g_ref, h_ref, after_ref, send_ref, keep_ref, held):
    del after_ref
    width = s_ref.shape[-1]
    half, part = width // 2, 64
    core = place_ref[3]

    @pl.when(pl.program_id(0) == 0)
    def _():
        for n, which in enumerate((1 - core, core)):
            lanes = pl.ds(pl.multiple_of(which * half, half), half)
            student = jnp.concatenate([x[:, 0, :, lanes].reshape(-1, half) for x in (s_ref, t_ref)], axis=0)
            held[n * half : (n + 1) * half, :] = student.T

    def columns(ref):
        parts = [ref[:, c * part : (c + 1) * part, :].reshape(-1, LANES) for c in range(2)]
        return jnp.concatenate(parts, axis=1)

    grad = jnp.concatenate([columns(g_ref), columns(h_ref)], axis=0)
    send_ref[...] = jnp.dot(held[:half, :], grad, preferred_element_type=f32)
    keep_ref[...] = jnp.dot(held[half:, :], grad, preferred_element_type=f32)


def finish(terms_ref, after_ref, o_ref, loss_ref):
    del after_ref
    total = jnp.zeros(terms_ref.shape[1:], f32)[:256]
    loss = jnp.zeros((1, LANES), f32)
    for n in range(terms_ref.shape[0]):
        meta = terms_ref[n, 256:, :]
        total = total + terms_ref[n, :256, :] * jnp.exp2(meta[:1] - TOP)
        loss = loss + (meta[2:3] + (meta[3:4] + meta[4:5] / 2048.0) / 2048.0) * jnp.exp2(meta[1:2] - 10.0)
    loss_ref[...] = loss
    for c in range(4):
        o_ref[:, c * LANES : (c + 1) * LANES] = total[64 * c : 64 * c + 64].astype(bf16)


def body(student_hidden, teacher_hidden, proj_weight):
    width_local = student_hidden.shape[3]
    student = student_hidden.reshape(-1, width_local)
    tokens, columns = student.shape[0], proj_weight.shape[1]
    tensor_count, dp_count, seq_count = (lax.axis_size(a) for a in ("tensor", "dp", "seq"))
    own = tokens // tensor_count
    blocks = columns // LANES

    dp_index = lax.axis_index("dp").astype(jnp.int32)
    core = (lax.axis_index("seq") % 2).astype(jnp.int32)
    place = jnp.stack([dp_index // 4, dp_index % 4, dp_index % 2, core])
    scalars = pl.BlockSpec(memory_space=pltpu.SMEM)
    whole = pl.BlockSpec(memory_space=pltpu.VMEM)

    with jax.named_scope("teacher"):
        spread = all_to_all(teacher_hidden.reshape(8, 8, -1), "tensor")
        group = (jax.ShapeDtypeStruct((64, columns // 2 + LANES), bf16),) * 4
        packed = call(
            pack_teacher,
            group,
            0,
            600_000,
            in_specs=[scalars, whole],
            out_specs=(whole,) * 4,
            scratch_shapes=[pltpu.VMEM((4, 64, columns // 2 + LANES), bf16)],
        )(place, spread.reshape(64, -1))
        near = [packed[0]]
        for k in range(1, 4):
            moves = [(z, (z + (k if k < 3 else -1)) % dp_count) for z in range(dp_count)]
            near.append(lax.ppermute(packed[k], "dp", moves))
        packed = call(
            regroup_teacher,
            group,
            0,
            600_000,
            in_specs=[scalars] + [whole] * 4,
            out_specs=(whole,) * 4,
        )(place, *near)
        target = [packed[0]]
        for m in range(1, 4):
            moves = [(z, (z + 4 * m) % dp_count) for z in range(dp_count)]
            target.append(lax.ppermute(packed[m], "dp", moves))

    with jax.named_scope("prediction"):
        size = blocks * own + META
        partial = call(
            forward,
            jax.ShapeDtypeStruct((tensor_count, size, LANES), f32),
            2 * tokens * width_local * columns,
            6_000_000,
            grid=(tensor_count // 2,),
            in_specs=[
                pl.BlockSpec((2 * own, width_local), lambda i: (i, 0)),
                pl.BlockSpec((width_local, columns), lambda i: (0, 0)),
            ],
            out_specs=pl.BlockSpec((2, size, LANES), lambda i: (i, 0, 0)),
        )(student, proj_weight)
        parts = all_to_all(partial.astype(f16), "tensor").astype(f32)
        unscale = jnp.exp2(parts[:, blocks * own, :] - TOP)
        data = parts[:, : blocks * own, :].reshape(tensor_count, blocks, own, LANES)
        prediction = jnp.sum(data * unscale[:, None, :, None], axis=0)

    with jax.named_scope("gradient"):
        part = blocks * own // 2
        block_a = pl.BlockSpec((1, part + PIECES, LANES), lambda i: (i, 0, 0))
        block_b = pl.BlockSpec((1, part, LANES), lambda i: (i, 0, 0))
        own_a, own_b = call(
            token_grad,
            (
                jax.ShapeDtypeStruct((tensor_count, part + PIECES, LANES), bf16),
                jax.ShapeDtypeStruct((tensor_count, part, LANES), bf16),
            ),
            2 * own * own * columns,
            3_000_000,
            grid=(tensor_count,),
            in_specs=[scalars, pl.BlockSpec((blocks, own, LANES), lambda i: (0, 0, 0))]
            + [pl.BlockSpec(group[0].shape, lambda i: (0, 0))] * 4,
            out_specs=(block_a, block_b),
            scratch_shapes=[pltpu.VMEM((blocks * own + PIECES, LANES), bf16)],
        )(place, prediction, *target)
        grad_a = all_to_all(own_a, "tensor")
        grad_b = all_to_all(own_b, "tensor")

    with jax.named_scope("input_grad"):
        chunk = 64 * 4 + META
        dp_half = dp_count // 2
        half_terms = jax.ShapeDtypeStruct((dp_half, chunk, LANES), f32)
        weights = pl.BlockSpec((width_local, columns), lambda i: (0, 0))
        losses = pl.BlockSpec((1, LANES), lambda i: (0, 0))
        block = pl.BlockSpec((4, chunk, LANES), lambda i: (i, 0, 0))
        send, total = call(
            send_terms,
            (half_terms, jax.ShapeDtypeStruct((1, LANES), f32)),
            tokens * width_local * columns,
            4_000_000,
            grid=(2,),
            in_specs=[
                pl.BlockSpec((4, part + PIECES, LANES), lambda i: (i, 0, 0)),
                weights,
                pl.BlockSpec((tensor_count, PIECES, LANES), lambda i: (0, part // PIECES, 0)),
            ],
            out_specs=(block, losses),
        )(grad_a, proj_weight, grad_a)
        neighbour = [(z, z ^ 1) for z in range(dp_count)]
        loss = butterfly(total, (("seq", 1), ("seq", 2), ("dp", 1)))
        got = lax.ppermute(send.astype(f16), "dp", neighbour).astype(f32)
        term = call(
            keep_terms,
            half_terms,
            tokens * width_local * columns,
            5_000_000,
            grid=(2,),
            in_specs=[pl.BlockSpec((4, part, LANES), lambda i: (i, 0, 0)), weights, block, losses],
            out_specs=block,
        )(grad_b, proj_weight, got, loss)
        same_parity = [list(range(p, dp_count, 2)) for p in range(2)]
        terms = lax.all_to_all(term.astype(f16), "dp", 0, 0, axis_index_groups=same_parity).astype(f32)

    with jax.named_scope("weight_grad"):
        other_core = [(i, i ^ 1) for i in range(seq_count)]
        other_y = [(i, i ^ 2) for i in range(seq_count)]
        half = jax.ShapeDtypeStruct((width_local // 2, columns), f32)
        by_chunk = student.reshape(8, 2, 64, width_local)
        send, keep = call(
            weight_grad,
            (half, half),
            2 * tokens * width_local * columns,
            5_000_000,
            grid_spec=pltpu.PrefetchScalarGridSpec(
                num_scalar_prefetch=1,
                grid=(4,),
                in_specs=[
                    pl.BlockSpec((8, 1, 64, width_local), lambda i, p: (0, 1 - p[2], 0, 0)),
                    pl.BlockSpec((8, 1, 64, width_local), lambda i, p: (0, p[2], 0, 0)),
                    pl.BlockSpec((tensor_count, own, LANES), lambda i, p: (0, i, 0)),
                    pl.BlockSpec((tensor_count, own, LANES), lambda i, p: (0, i, 0)),
                    pl.BlockSpec((1, META, LANES), lambda i, p: (0, 256 // META, 0)),
                ],
                out_specs=(
                    pl.BlockSpec((width_local // 2, 2 * LANES), lambda i, p: (0, i)),
                    pl.BlockSpec((width_local // 2, 2 * LANES), lambda i, p: (0, i)),
                ),
                scratch_shapes=[pltpu.VMEM((width_local, tokens), bf16)],
            ),
        )(place, by_chunk, by_chunk, grad_a, grad_b, term)
        pair = (keep + lax.ppermute(send, "seq", other_core)).astype(bf16)
        mine = pair.astype(f32) + lax.ppermute(pair, "seq", other_y).astype(f32)
        theirs = lax.ppermute(mine, "seq", other_core)
        grad_weight = jnp.where(
            core == 0,
            jnp.concatenate([mine, theirs], axis=0),
            jnp.concatenate([theirs, mine], axis=0),
        )

    with jax.named_scope("results"):
        grad_input, loss = call(
            finish,
            (jax.ShapeDtypeStruct((own // 2, width_local), bf16), jax.ShapeDtypeStruct((1, LANES), f32)),
            0,
            1_200_000,
            grid=(1,),
            in_specs=[
                pl.BlockSpec((dp_half, chunk, LANES), lambda i: (0, 0, 0)),
                pl.BlockSpec((8, LANES), lambda i: (0, 0)),
            ],
            out_specs=(
                pl.BlockSpec((own // 2, width_local), lambda i: (0, 0)),
                pl.BlockSpec((1, LANES), lambda i: (0, 0)),
            ),
        )(terms, grad_weight)
        grad_input = grad_input.reshape(1, 4, 16, width_local)
        loss_value = loss[0, 0] / (tokens * seq_count * columns * dp_count)
    return (loss_value, grad_weight, grad_input)


def solution(mesh):
    placed = (P("seq", None, None, "tensor"), P("seq", None, "dp", "tensor"), P("tensor", "dp"))
    return jax.shard_map(
        body,
        mesh=mesh,
        in_specs=placed,
        out_specs=(P(), P("tensor", "dp"), P("seq", "dp", None, "tensor")),
        check_vma=False,
    )
```

```python
import jax
import jax.numpy as jnp
from jax import lax
from jax.experimental import pallas as pl
from jax.experimental.pallas import tpu as pltpu
from jax.sharding import PartitionSpec as P

scale_epsilon = 1e-06
grad_factor = 0.25
LANES = 128
META = 8
PIECES = 16
TOP = 14.0
WAITS = 30_000_000_000
bf16, f16, f32 = jnp.bfloat16, jnp.float16, jnp.float32


def call(kernel, out_shape, flops, nbytes, **kw):
    return pl.pallas_call(
        kernel,
        out_shape=out_shape,
        cost_estimate=pl.CostEstimate(flops=flops, bytes_accessed=nbytes, transcendentals=0),
        compiler_params=pltpu.CompilerParams(vmem_limit_bytes=16 * 1024 * 1024),
        **kw,
    )


def all_to_all(x, axis):
    return lax.all_to_all(x, axis, 0, 0)


def butterfly(x, steps):
    for axis, step in steps:
        x = x + lax.ppermute(x, axis, [(i, i ^ step) for i in range(lax.axis_size(axis))])
    return x


def exponent_of(largest):
    return jnp.clip(jnp.ceil(jnp.log2(jnp.maximum(largest, 1e-30))), -100.0, 100.0)


def pack_teacher(place_ref, x_ref, after_ref, *refs):
    del after_ref
    held = refs[4]
    rows = x_ref[...].astype(f32)
    largest = jnp.max(jnp.max(jnp.abs(rows).reshape(8, 8, -1), axis=0), axis=1, keepdims=True)
    wide = jnp.broadcast_to(jnp.concatenate([largest, largest], axis=0), (16, LANES)).astype(bf16)
    half = rows.shape[1] // 4
    for t in range(8):
        for j in range(2):
            block = rows[8 * t : 8 * t + 8, 2 * half * j : 2 * half * (j + 1)]
            both = jnp.concatenate([block[:, :half], block[:, half:]], axis=0)
            low, high = 2 * (t % 2) + j, t // 2
            held[low, 16 * high : 16 * high + 16, :half] = both.astype(bf16)
            held[low, 16 * high : 16 * high + 16, half:] = wide
    for k in range(4):
        refs[k][...] = held[(place_ref[1] + k) & 3]


def regroup_teacher(place_ref, *refs):
    for m in range(4):
        high = (place_ref[0] + m) & 3
        for k in range(4):
            refs[4 + m][16 * k : 16 * k + 16, :] = refs[k][pl.ds(pl.multiple_of(16 * high, 16), 16), :]


def forward(s_ref, w_ref, o_ref):
    partial = jnp.dot(s_ref[...], w_ref[...], preferred_element_type=f32)
    power = exponent_of(jnp.max(jnp.abs(partial), axis=1, keepdims=True))
    scaled = partial * jnp.exp2(TOP - power)
    rows, width = scaled.shape[0] // 2, scaled.shape[1]
    for n in range(2):
        for c in range(width // LANES):
            o_ref[n, c * rows : (c + 1) * rows, :] = scaled[n * rows : (n + 1) * rows, c * LANES : (c + 1) * LANES]
        meta = jnp.transpose(jnp.broadcast_to(power[n * rows : (n + 1) * rows], (rows, LANES)))
        o_ref[n, width // LANES * rows :, :] = meta[:META]


def token_grad(place_ref, pred_ref, t0_ref, t1_ref, t2_ref, t3_ref, a_ref, b_ref, held):
    blocks, rows, _ = pred_ref.shape

    @pl.when(pl.program_id(0) == 0)
    def _():
        arrived = jnp.concatenate([t0_ref[...], t1_ref[...], t2_ref[...], t3_ref[...]], axis=0)
        count, half = arrived.shape[0], blocks // 2 * LANES
        r = lax.broadcasted_iota(jnp.int32, (rows, count), 0)
        q = lax.broadcasted_iota(jnp.int32, (rows, count), 1)
        shift = q // 16 % 4
        shift = jnp.where(shift == 3, -1, shift)
        second = (place_ref[0] * 4 + place_ref[1] - 4 * (q // 64) - shift) & 15
        match = r == (q % 8) * 16 + second
        first = jnp.where(match & (q // 8 % 2 == 0), 1.0, 0.0).astype(bf16)
        other = jnp.where(match & (q // 8 % 2 == 1), 1.0, 0.0).astype(bf16)
        left = jnp.dot(first, arrived, preferred_element_type=f32)
        right = jnp.dot(other, arrived[:, :half], preferred_element_type=f32)
        target = jnp.concatenate([left[:, :half], right], axis=1)
        token_scale = left[:, half : half + 1] + scale_epsilon
        total = jnp.zeros((rows, LANES), f32)
        for c in range(blocks):
            quantized = (target[:, c * LANES : (c + 1) * LANES] / token_scale).astype(bf16)
            difference = pred_ref[c] / token_scale - quantized.astype(f32)
            total = total + difference * difference
            held[c * rows : (c + 1) * rows, :] = ((difference / token_scale) * grad_factor).astype(bf16)
        loss = jnp.sum(jnp.sum(total, axis=0, keepdims=True), axis=1, keepdims=True)
        high = loss.astype(bf16).astype(f32)
        middle = (loss - high).astype(bf16).astype(f32)
        low = loss - high - middle
        row = lax.broadcasted_iota(jnp.int32, (PIECES, LANES), 0)
        pieces = jnp.where(row == 0, high, jnp.where(row == 1, middle, jnp.where(row == 2, low, 0.0)))
        held[blocks * rows :, :] = pieces.astype(bf16)

    part = rows // 2
    for ref, chunk in ((a_ref, 1 - place_ref[2]), (b_ref, place_ref[2])):
        for c in range(blocks):
            start = pl.multiple_of(c * rows + chunk * part, part)
            ref[0, c * part : (c + 1) * part, :] = held[pl.ds(start, part), :]
    a_ref[0, blocks * part :, :] = held[blocks * rows :, :]


def scaled_by_power(chunk):
    largest = jnp.max(jnp.max(jnp.abs(chunk), axis=0, keepdims=True), axis=1, keepdims=True)
    power = exponent_of(largest)
    return chunk * jnp.exp2(TOP - power), power


def loss_rows(loss):
    row = lax.broadcasted_iota(jnp.int32, (META, LANES), 0)
    power = exponent_of(loss)
    scaled = loss * jnp.exp2(10.0 - power)
    high = jnp.floor(scaled)
    rest = (scaled - high) * 2048.0
    middle = jnp.floor(rest)
    low = jnp.floor((rest - middle) * 2048.0)
    return row, jnp.where(row == 1, power, jnp.where(row == 2, high, jnp.where(row == 3, middle, low)))


def chunk_terms(g_ref, w_ref):
    part = 64
    grad = jnp.concatenate(
        [
            jnp.concatenate([g_ref[n, c * part : (c + 1) * part, :] for c in range(8)], axis=1)
            for n in range(g_ref.shape[0])
        ],
        axis=0,
    )
    terms = lax.dot_general(grad, w_ref[...], (((1,), (1,)), ((), ())), preferred_element_type=f32)
    return [terms[n * part : (n + 1) * part] for n in range(g_ref.shape[0])]


def send_terms(g_ref, w_ref, loss_ref, send_ref, total_ref):
    pieces = jnp.sum(loss_ref[...].astype(f32), axis=0)
    total_ref[...] = jnp.sum(pieces, axis=0, keepdims=True)
    for n, chunk in enumerate(chunk_terms(g_ref, w_ref)):
        scaled, power = scaled_by_power(chunk)
        for c in range(4):
            send_ref[n, 64 * c : 64 * c + 64, :] = scaled[:, c * LANES : (c + 1) * LANES]
        send_ref[n, 256:, :] = jnp.broadcast_to(power, (META, LANES))


def keep_terms(g_ref, w_ref, got_ref, loss_ref, o_ref):
    row, meta = loss_rows(loss_ref[...])
    for n, chunk in enumerate(chunk_terms(g_ref, w_ref)):
        got = jnp.concatenate([got_ref[n, 64 * c : 64 * c + 64, :] for c in range(4)], axis=1)
        chunk = chunk + got * jnp.exp2(got_ref[n, 256:257, 0:1] - TOP)
        scaled, power = scaled_by_power(chunk)
        for c in range(4):
            o_ref[n, 64 * c : 64 * c + 64, :] = scaled[:, c * LANES : (c + 1) * LANES]
        o_ref[n, 256:, :] = jnp.where(row == 0, power, meta)


def weight_grad(place_ref, s_ref, t_ref, g_ref, h_ref, after_ref, send_ref, keep_ref, held):
    del after_ref
    width = s_ref.shape[-1]
    half, part = width // 2, 64
    core = place_ref[3]

    @pl.when(pl.program_id(0) == 0)
    def _():
        for n, which in enumerate((1 - core, core)):
            lanes = pl.ds(pl.multiple_of(which * half, half), half)
            student = jnp.concatenate([x[:, 0, :, lanes].reshape(-1, half) for x in (s_ref, t_ref)], axis=0)
            held[n * half : (n + 1) * half, :] = student.T

    def columns(ref):
        parts = [ref[:, c * part : (c + 1) * part, :].reshape(-1, LANES) for c in range(2)]
        return jnp.concatenate(parts, axis=1)

    grad = jnp.concatenate([columns(g_ref), columns(h_ref)], axis=0)
    send_ref[...] = jnp.dot(held[:half, :], grad, preferred_element_type=f32)
    keep_ref[...] = jnp.dot(held[half:, :], grad, preferred_element_type=f32)


def finish(terms_ref, after_ref, o_ref, loss_ref):
    del after_ref
    total = jnp.zeros(terms_ref.shape[1:], f32)[:256]
    loss = jnp.zeros((1, LANES), f32)
    for n in range(terms_ref.shape[0]):
        meta = terms_ref[n, 256:, :]
        total = total + terms_ref[n, :256, :] * jnp.exp2(meta[:1] - TOP)
        loss = loss + (meta[2:3] + (meta[3:4] + meta[4:5] / 2048.0) / 2048.0) * jnp.exp2(meta[1:2] - 10.0)
    loss_ref[...] = loss
    for c in range(4):
        o_ref[:, c * LANES : (c + 1) * LANES] = total[64 * c : 64 * c + 64].astype(bf16)


def body(student_hidden, teacher_hidden, proj_weight):
    width_local = student_hidden.shape[3]
    student = student_hidden.reshape(-1, width_local)
    tokens, columns = student.shape[0], proj_weight.shape[1]
    tensor_count, dp_count, seq_count = (lax.axis_size(a) for a in ("tensor", "dp", "seq"))
    own = tokens // tensor_count
    blocks = columns // LANES

    dp_index = lax.axis_index("dp").astype(jnp.int32)
    core = (lax.axis_index("seq") % 2).astype(jnp.int32)
    place = jnp.stack([dp_index // 4, dp_index % 4, dp_index % 2, core])
    scalars = pl.BlockSpec(memory_space=pltpu.SMEM)
    whole = pl.BlockSpec(memory_space=pltpu.VMEM)

    with jax.named_scope("teacher"):
        spread = all_to_all(teacher_hidden.reshape(8, 8, -1), "tensor")
        size = blocks * own + META
        partial = call(
            forward,
            jax.ShapeDtypeStruct((tensor_count, size, LANES), f32),
            2 * tokens * width_local * columns,
            6_000_000,
            grid=(tensor_count // 2,),
            in_specs=[
                pl.BlockSpec((2 * own, width_local), lambda i: (i, 0)),
                pl.BlockSpec((width_local, columns), lambda i: (0, 0)),
            ],
            out_specs=pl.BlockSpec((2, size, LANES), lambda i: (i, 0, 0)),
        )(student, proj_weight)
        partial = partial.astype(f16)
        group = (jax.ShapeDtypeStruct((64, columns // 2 + LANES), bf16),) * 4
        packed = call(
            pack_teacher,
            group,
            0,
            600_000,
            grid=(1,),
            in_specs=[
                scalars,
                pl.BlockSpec((64, 2 * columns), lambda i: (0, 0)),
                pl.BlockSpec((META, LANES), lambda i: (0, 0)),
            ],
            out_specs=(pl.BlockSpec(group[0].shape, lambda i: (0, 0)),) * 4,
            scratch_shapes=[pltpu.VMEM((4, 64, columns // 2 + LANES), bf16)],
        )(place, spread.reshape(64, -1), partial[0, :META, :].astype(f32))
        near = [packed[0]]
        for k in range(1, 4):
            moves = [(z, (z + (k if k < 3 else -1)) % dp_count) for z in range(dp_count)]
            near.append(lax.ppermute(packed[k], "dp", moves))
        packed = call(
            regroup_teacher,
            group,
            WAITS,
            600_000,
            in_specs=[scalars] + [whole] * 4,
            out_specs=(whole,) * 4,
        )(place, *near)
        target = [packed[0]]
        for m in range(1, 4):
            moves = [(z, (z + 4 * m) % dp_count) for z in range(dp_count)]
            target.append(lax.ppermute(packed[m], "dp", moves))

    with jax.named_scope("prediction"):
        parts = all_to_all(partial, "tensor").astype(f32)
        unscale = jnp.exp2(parts[:, blocks * own, :] - TOP)
        data = parts[:, : blocks * own, :].reshape(tensor_count, blocks, own, LANES)
        prediction = jnp.sum(data * unscale[:, None, :, None], axis=0)

    with jax.named_scope("gradient"):
        part = blocks * own // 2
        block_a = pl.BlockSpec((1, part + PIECES, LANES), lambda i: (i, 0, 0))
        block_b = pl.BlockSpec((1, part, LANES), lambda i: (i, 0, 0))
        own_a, own_b = call(
            token_grad,
            (
                jax.ShapeDtypeStruct((tensor_count, part + PIECES, LANES), bf16),
                jax.ShapeDtypeStruct((tensor_count, part, LANES), bf16),
            ),
            2 * own * own * columns,
            3_000_000,
            grid=(tensor_count,),
            in_specs=[scalars, pl.BlockSpec((blocks, own, LANES), lambda i: (0, 0, 0))]
            + [pl.BlockSpec(group[0].shape, lambda i: (0, 0))] * 4,
            out_specs=(block_a, block_b),
            scratch_shapes=[pltpu.VMEM((blocks * own + PIECES, LANES), bf16)],
        )(place, prediction, *target)
        grad_a = all_to_all(own_a, "tensor")
        grad_b = all_to_all(own_b, "tensor")

    with jax.named_scope("input_grad"):
        chunk = 64 * 4 + META
        dp_half = dp_count // 2
        half_terms = jax.ShapeDtypeStruct((dp_half, chunk, LANES), f32)
        weights = pl.BlockSpec((width_local, columns), lambda i: (0, 0))
        losses = pl.BlockSpec((1, LANES), lambda i: (0, 0))
        block = pl.BlockSpec((4, chunk, LANES), lambda i: (i, 0, 0))
        send, total = call(
            send_terms,
            (half_terms, jax.ShapeDtypeStruct((1, LANES), f32)),
            tokens * width_local * columns,
            4_000_000,
            grid=(2,),
            in_specs=[
                pl.BlockSpec((4, part + PIECES, LANES), lambda i: (i, 0, 0)),
                weights,
                pl.BlockSpec((tensor_count, PIECES, LANES), lambda i: (0, part // PIECES, 0)),
            ],
            out_specs=(block, losses),
        )(grad_a, proj_weight, grad_a)
        neighbour = [(z, z ^ 1) for z in range(dp_count)]
        loss = butterfly(total, (("seq", 1), ("seq", 2), ("dp", 1)))
        got = lax.ppermute(send.astype(f16), "dp", neighbour).astype(f32)
        term = call(
            keep_terms,
            half_terms,
            tokens * width_local * columns,
            5_000_000,
            grid=(2,),
            in_specs=[pl.BlockSpec((4, part, LANES), lambda i: (i, 0, 0)), weights, block, losses],
            out_specs=block,
        )(grad_b, proj_weight, got, loss)
        same_parity = [list(range(p, dp_count, 2)) for p in range(2)]
        terms = lax.all_to_all(term.astype(f16), "dp", 0, 0, axis_index_groups=same_parity).astype(f32)

    with jax.named_scope("weight_grad"):
        other_core = [(i, i ^ 1) for i in range(seq_count)]
        other_y = [(i, i ^ 2) for i in range(seq_count)]
        half = jax.ShapeDtypeStruct((width_local // 2, columns), f32)
        by_chunk = student.reshape(8, 2, 64, width_local)
        send, keep = call(
            weight_grad,
            (half, half),
            2 * tokens * width_local * columns,
            5_000_000,
            grid_spec=pltpu.PrefetchScalarGridSpec(
                num_scalar_prefetch=1,
                grid=(4,),
                in_specs=[
                    pl.BlockSpec((8, 1, 64, width_local), lambda i, p: (0, 1 - p[2], 0, 0)),
                    pl.BlockSpec((8, 1, 64, width_local), lambda i, p: (0, p[2], 0, 0)),
                    pl.BlockSpec((tensor_count, own, LANES), lambda i, p: (0, i, 0)),
                    pl.BlockSpec((tensor_count, own, LANES), lambda i, p: (0, i, 0)),
                    pl.BlockSpec((1, META, LANES), lambda i, p: (0, 256 // META, 0)),
                ],
                out_specs=(
                    pl.BlockSpec((width_local // 2, 2 * LANES), lambda i, p: (0, i)),
                    pl.BlockSpec((width_local // 2, 2 * LANES), lambda i, p: (0, i)),
                ),
                scratch_shapes=[pltpu.VMEM((width_local, tokens), bf16)],
            ),
        )(place, by_chunk, by_chunk, grad_a, grad_b, term)
        pair = (keep + lax.ppermute(send, "seq", other_core)).astype(bf16)
        mine = pair.astype(f32) + lax.ppermute(pair, "seq", other_y).astype(f32)
        theirs = lax.ppermute(mine, "seq", other_core)
        grad_weight = jnp.where(
            core == 0,
            jnp.concatenate([mine, theirs], axis=0),
            jnp.concatenate([theirs, mine], axis=0),
        )

    with jax.named_scope("results"):
        grad_input, loss = call(
            finish,
            (jax.ShapeDtypeStruct((own // 2, width_local), bf16), jax.ShapeDtypeStruct((1, LANES), f32)),
            0,
            1_200_000,
            grid=(1,),
            in_specs=[
                pl.BlockSpec((dp_half, chunk, LANES), lambda i: (0, 0, 0)),
                pl.BlockSpec((8, LANES), lambda i: (0, 0)),
            ],
            out_specs=(
                pl.BlockSpec((own // 2, width_local), lambda i: (0, 0)),
                pl.BlockSpec((1, LANES), lambda i: (0, 0)),
            ),
        )(terms, grad_weight)
        grad_input = grad_input.reshape(1, 4, 16, width_local)
        loss_value = loss[0, 0] / (tokens * seq_count * columns * dp_count)
    return (loss_value, grad_weight, grad_input)


def solution(mesh):
    placed = (P("seq", None, None, "tensor"), P("seq", None, "dp", "tensor"), P("tensor", "dp"))
    return jax.shard_map(
        body,
        mesh=mesh,
        in_specs=placed,
        out_specs=(P(), P("tensor", "dp"), P("seq", "dp", None, "tensor")),
        check_vma=False,
    )
```

```python
import jax
import jax.numpy as jnp
from jax import lax
from jax.experimental import pallas as pl
from jax.experimental.pallas import tpu as pltpu
from jax.sharding import PartitionSpec as P

scale_epsilon = 1e-06
grad_factor = 0.25
LANES = 128
META = 8
PIECES = 16
TOP = 14.0
WAITS = 30_000_000_000
bf16, f16, f32 = jnp.bfloat16, jnp.float16, jnp.float32


def call(kernel, out_shape, flops, nbytes, **kw):
    return pl.pallas_call(
        kernel,
        out_shape=out_shape,
        cost_estimate=pl.CostEstimate(flops=flops, bytes_accessed=nbytes, transcendentals=0),
        compiler_params=pltpu.CompilerParams(vmem_limit_bytes=16 * 1024 * 1024),
        **kw,
    )


def all_to_all(x, axis):
    return lax.all_to_all(x, axis, 0, 0)


def butterfly(x, steps):
    for axis, step in steps:
        x = x + lax.ppermute(x, axis, [(i, i ^ step) for i in range(lax.axis_size(axis))])
    return x


def exponent_of(largest):
    return jnp.clip(jnp.ceil(jnp.log2(jnp.maximum(largest, 1e-30))), -100.0, 100.0)


def pack_teacher(place_ref, x_ref, after_ref, *refs):
    del after_ref
    held = refs[4]
    rows = x_ref[...].astype(f32)
    largest = jnp.max(jnp.max(jnp.abs(rows).reshape(8, 8, -1), axis=0), axis=1, keepdims=True)
    wide = jnp.broadcast_to(jnp.concatenate([largest, largest], axis=0), (16, LANES)).astype(bf16)
    half = rows.shape[1] // 4
    for t in range(8):
        for j in range(2):
            block = rows[8 * t : 8 * t + 8, 2 * half * j : 2 * half * (j + 1)]
            both = jnp.concatenate([block[:, :half], block[:, half:]], axis=0)
            low, high = 2 * (t % 2) + j, t // 2
            held[low, 16 * high : 16 * high + 16, :half] = both.astype(bf16)
            held[low, 16 * high : 16 * high + 16, half:] = wide
    for k in range(4):
        refs[k][...] = held[(place_ref[1] + k) & 3]


def regroup_teacher(place_ref, *refs):
    for m in range(4):
        high = (place_ref[0] + m) & 3
        for k in range(4):
            refs[4 + m][16 * k : 16 * k + 16, :] = refs[k][pl.ds(pl.multiple_of(16 * high, 16), 16), :]


def forward(s_ref, w_ref, o_ref, done_ref):
    done_ref[...] = jnp.zeros_like(done_ref)
    partial = jnp.dot(s_ref[...], w_ref[...], preferred_element_type=f32)
    power = exponent_of(jnp.max(jnp.abs(partial), axis=1, keepdims=True))
    scaled = partial * jnp.exp2(TOP - power)
    rows, width = scaled.shape[0] // 2, scaled.shape[1]
    for n in range(2):
        for c in range(width // LANES):
            o_ref[n, c * rows : (c + 1) * rows, :] = scaled[n * rows : (n + 1) * rows, c * LANES : (c + 1) * LANES]
        meta = jnp.transpose(jnp.broadcast_to(power[n * rows : (n + 1) * rows], (rows, LANES)))
        o_ref[n, width // LANES * rows :, :] = meta[:META]


def token_grad(place_ref, pred_ref, t0_ref, t1_ref, t2_ref, t3_ref, a_ref, b_ref, held):
    blocks, rows, _ = pred_ref.shape

    @pl.when(pl.program_id(0) == 0)
    def _():
        arrived = jnp.concatenate([t0_ref[...], t1_ref[...], t2_ref[...], t3_ref[...]], axis=0)
        count, half = arrived.shape[0], blocks // 2 * LANES
        r = lax.broadcasted_iota(jnp.int32, (rows, count), 0)
        q = lax.broadcasted_iota(jnp.int32, (rows, count), 1)
        shift = q // 16 % 4
        shift = jnp.where(shift == 3, -1, shift)
        second = (place_ref[0] * 4 + place_ref[1] - 4 * (q // 64) - shift) & 15
        match = r == (q % 8) * 16 + second
        first = jnp.where(match & (q // 8 % 2 == 0), 1.0, 0.0).astype(bf16)
        other = jnp.where(match & (q // 8 % 2 == 1), 1.0, 0.0).astype(bf16)
        left = jnp.dot(first, arrived, preferred_element_type=f32)
        right = jnp.dot(other, arrived[:, :half], preferred_element_type=f32)
        target = jnp.concatenate([left[:, :half], right], axis=1)
        token_scale = left[:, half : half + 1] + scale_epsilon
        total = jnp.zeros((rows, LANES), f32)
        for c in range(blocks):
            quantized = (target[:, c * LANES : (c + 1) * LANES] / token_scale).astype(bf16)
            difference = pred_ref[c] / token_scale - quantized.astype(f32)
            total = total + difference * difference
            held[c * rows : (c + 1) * rows, :] = ((difference / token_scale) * grad_factor).astype(bf16)
        loss = jnp.sum(jnp.sum(total, axis=0, keepdims=True), axis=1, keepdims=True)
        high = loss.astype(bf16).astype(f32)
        middle = (loss - high).astype(bf16).astype(f32)
        low = loss - high - middle
        row = lax.broadcasted_iota(jnp.int32, (PIECES, LANES), 0)
        pieces = jnp.where(row == 0, high, jnp.where(row == 1, middle, jnp.where(row == 2, low, 0.0)))
        held[blocks * rows :, :] = pieces.astype(bf16)

    part = rows // 2
    for ref, chunk in ((a_ref, 1 - place_ref[2]), (b_ref, place_ref[2])):
        for c in range(blocks):
            start = pl.multiple_of(c * rows + chunk * part, part)
            ref[0, c * part : (c + 1) * part, :] = held[pl.ds(start, part), :]
    a_ref[0, blocks * part :, :] = held[blocks * rows :, :]


def scaled_by_power(chunk):
    largest = jnp.max(jnp.max(jnp.abs(chunk), axis=0, keepdims=True), axis=1, keepdims=True)
    power = exponent_of(largest)
    return chunk * jnp.exp2(TOP - power), power


def loss_rows(loss):
    row = lax.broadcasted_iota(jnp.int32, (META, LANES), 0)
    power = exponent_of(loss)
    scaled = loss * jnp.exp2(10.0 - power)
    high = jnp.floor(scaled)
    rest = (scaled - high) * 2048.0
    middle = jnp.floor(rest)
    low = jnp.floor((rest - middle) * 2048.0)
    return row, jnp.where(row == 1, power, jnp.where(row == 2, high, jnp.where(row == 3, middle, low)))


def chunk_terms(g_ref, w_ref):
    part = 64
    grad = jnp.concatenate(
        [
            jnp.concatenate([g_ref[n, c * part : (c + 1) * part, :] for c in range(8)], axis=1)
            for n in range(g_ref.shape[0])
        ],
        axis=0,
    )
    terms = lax.dot_general(grad, w_ref[...], (((1,), (1,)), ((), ())), preferred_element_type=f32)
    return [terms[n * part : (n + 1) * part] for n in range(g_ref.shape[0])]


def send_terms(g_ref, w_ref, loss_ref, send_ref, total_ref):
    pieces = jnp.sum(loss_ref[...].astype(f32), axis=0)
    total_ref[...] = jnp.sum(pieces, axis=0, keepdims=True)
    for n, chunk in enumerate(chunk_terms(g_ref, w_ref)):
        scaled, power = scaled_by_power(chunk)
        for c in range(4):
            send_ref[n, 64 * c : 64 * c + 64, :] = scaled[:, c * LANES : (c + 1) * LANES]
        send_ref[n, 256:, :] = jnp.broadcast_to(power, (META, LANES))


def keep_terms(g_ref, w_ref, got_ref, loss_ref, o_ref):
    row, meta = loss_rows(loss_ref[...])
    for n, chunk in enumerate(chunk_terms(g_ref, w_ref)):
        got = jnp.concatenate([got_ref[n, 64 * c : 64 * c + 64, :] for c in range(4)], axis=1)
        chunk = chunk + got * jnp.exp2(got_ref[n, 256:257, 0:1] - TOP)
        scaled, power = scaled_by_power(chunk)
        for c in range(4):
            o_ref[n, 64 * c : 64 * c + 64, :] = scaled[:, c * LANES : (c + 1) * LANES]
        o_ref[n, 256:, :] = jnp.where(row == 0, power, meta)


def weight_grad(place_ref, s_ref, t_ref, g_ref, h_ref, after_ref, send_ref, keep_ref, held):
    del after_ref
    width = s_ref.shape[-1]
    half, part = width // 2, 64
    core = place_ref[3]

    @pl.when(pl.program_id(0) == 0)
    def _():
        for n, which in enumerate((1 - core, core)):
            lanes = pl.ds(pl.multiple_of(which * half, half), half)
            student = jnp.concatenate([x[:, 0, :, lanes].reshape(-1, half) for x in (s_ref, t_ref)], axis=0)
            held[n * half : (n + 1) * half, :] = student.T

    def columns(ref):
        parts = [ref[:, c * part : (c + 1) * part, :].reshape(-1, LANES) for c in range(2)]
        return jnp.concatenate(parts, axis=1)

    grad = jnp.concatenate([columns(g_ref), columns(h_ref)], axis=0)
    send_ref[...] = jnp.dot(held[:half, :], grad, preferred_element_type=f32)
    keep_ref[...] = jnp.dot(held[half:, :], grad, preferred_element_type=f32)


def finish(terms_ref, after_ref, o_ref, loss_ref):
    del after_ref
    total = jnp.zeros(terms_ref.shape[1:], f32)[:256]
    loss = jnp.zeros((1, LANES), f32)
    for n in range(terms_ref.shape[0]):
        meta = terms_ref[n, 256:, :]
        total = total + terms_ref[n, :256, :] * jnp.exp2(meta[:1] - TOP)
        loss = loss + (meta[2:3] + (meta[3:4] + meta[4:5] / 2048.0) / 2048.0) * jnp.exp2(meta[1:2] - 10.0)
    loss_ref[...] = loss
    for c in range(4):
        o_ref[:, c * LANES : (c + 1) * LANES] = total[64 * c : 64 * c + 64].astype(bf16)


def body(student_hidden, teacher_hidden, proj_weight):
    width_local = student_hidden.shape[3]
    student = student_hidden.reshape(-1, width_local)
    tokens, columns = student.shape[0], proj_weight.shape[1]
    tensor_count, dp_count, seq_count = (lax.axis_size(a) for a in ("tensor", "dp", "seq"))
    own = tokens // tensor_count
    blocks = columns // LANES

    dp_index = lax.axis_index("dp").astype(jnp.int32)
    core = (lax.axis_index("seq") % 2).astype(jnp.int32)
    place = jnp.stack([dp_index // 4, dp_index % 4, dp_index % 2, core])
    scalars = pl.BlockSpec(memory_space=pltpu.SMEM)
    whole = pl.BlockSpec(memory_space=pltpu.VMEM)

    with jax.named_scope("teacher"):
        spread = all_to_all(teacher_hidden.reshape(8, 8, -1), "tensor")
        size = blocks * own + META
        partial, done = call(
            forward,
            (
                jax.ShapeDtypeStruct((tensor_count, size, LANES), f32),
                jax.ShapeDtypeStruct((META, LANES), f32),
            ),
            2 * tokens * width_local * columns,
            6_000_000,
            grid=(tensor_count // 2,),
            in_specs=[
                pl.BlockSpec((2 * own, width_local), lambda i: (i, 0)),
                pl.BlockSpec((width_local, columns), lambda i: (0, 0)),
            ],
            out_specs=(
                pl.BlockSpec((2, size, LANES), lambda i: (i, 0, 0)),
                pl.BlockSpec((META, LANES), lambda i: (0, 0)),
            ),
        )(student, proj_weight)
        partial, done = lax.optimization_barrier((partial.astype(f16), done))
        group = (jax.ShapeDtypeStruct((64, columns // 2 + LANES), bf16),) * 4
        packed = call(
            pack_teacher,
            group,
            0,
            600_000,
            grid=(1,),
            in_specs=[
                scalars,
                pl.BlockSpec((64, 2 * columns), lambda i: (0, 0)),
                pl.BlockSpec((META, LANES), lambda i: (0, 0)),
            ],
            out_specs=(pl.BlockSpec(group[0].shape, lambda i: (0, 0)),) * 4,
            scratch_shapes=[pltpu.VMEM((4, 64, columns // 2 + LANES), bf16)],
        )(place, spread.reshape(64, -1), done)
        near = [packed[0]]
        for k in range(1, 4):
            moves = [(z, (z + (k if k < 3 else -1)) % dp_count) for z in range(dp_count)]
            near.append(lax.ppermute(packed[k], "dp", moves))
        packed = call(
            regroup_teacher,
            group,
            WAITS,
            600_000,
            in_specs=[scalars] + [whole] * 4,
            out_specs=(whole,) * 4,
        )(place, *near)
        target = [packed[0]]
        for m in range(1, 4):
            moves = [(z, (z + 4 * m) % dp_count) for z in range(dp_count)]
            target.append(lax.ppermute(packed[m], "dp", moves))

    with jax.named_scope("prediction"):
        parts = all_to_all(partial, "tensor").astype(f32)
        unscale = jnp.exp2(parts[:, blocks * own, :] - TOP)
        data = parts[:, : blocks * own, :].reshape(tensor_count, blocks, own, LANES)
        prediction = jnp.sum(data * unscale[:, None, :, None], axis=0)

    with jax.named_scope("gradient"):
        part = blocks * own // 2
        block_a = pl.BlockSpec((1, part + PIECES, LANES), lambda i: (i, 0, 0))
        block_b = pl.BlockSpec((1, part, LANES), lambda i: (i, 0, 0))
        own_a, own_b = call(
            token_grad,
            (
                jax.ShapeDtypeStruct((tensor_count, part + PIECES, LANES), bf16),
                jax.ShapeDtypeStruct((tensor_count, part, LANES), bf16),
            ),
            2 * own * own * columns,
            3_000_000,
            grid=(tensor_count,),
            in_specs=[scalars, pl.BlockSpec((blocks, own, LANES), lambda i: (0, 0, 0))]
            + [pl.BlockSpec(group[0].shape, lambda i: (0, 0))] * 4,
            out_specs=(block_a, block_b),
            scratch_shapes=[pltpu.VMEM((blocks * own + PIECES, LANES), bf16)],
        )(place, prediction, *target)
        grad_a = all_to_all(own_a, "tensor")
        grad_b = all_to_all(own_b, "tensor")

    with jax.named_scope("input_grad"):
        chunk = 64 * 4 + META
        dp_half = dp_count // 2
        half_terms = jax.ShapeDtypeStruct((dp_half, chunk, LANES), f32)
        weights = pl.BlockSpec((width_local, columns), lambda i: (0, 0))
        losses = pl.BlockSpec((1, LANES), lambda i: (0, 0))
        block = pl.BlockSpec((4, chunk, LANES), lambda i: (i, 0, 0))
        send, total = call(
            send_terms,
            (half_terms, jax.ShapeDtypeStruct((1, LANES), f32)),
            tokens * width_local * columns,
            4_000_000,
            grid=(2,),
            in_specs=[
                pl.BlockSpec((4, part + PIECES, LANES), lambda i: (i, 0, 0)),
                weights,
                pl.BlockSpec((tensor_count, PIECES, LANES), lambda i: (0, part // PIECES, 0)),
            ],
            out_specs=(block, losses),
        )(grad_a, proj_weight, grad_a)
        neighbour = [(z, z ^ 1) for z in range(dp_count)]
        loss = butterfly(total, (("seq", 1), ("seq", 2), ("dp", 1)))
        got = lax.ppermute(send.astype(f16), "dp", neighbour)
        got = lax.optimization_barrier((got, grad_b))[0].astype(f32)
        term = call(
            keep_terms,
            half_terms,
            tokens * width_local * columns,
            5_000_000,
            grid=(2,),
            in_specs=[pl.BlockSpec((4, part, LANES), lambda i: (i, 0, 0)), weights, block, losses],
            out_specs=block,
        )(grad_b, proj_weight, got, loss)
        same_parity = [list(range(p, dp_count, 2)) for p in range(2)]
        terms = lax.all_to_all(term.astype(f16), "dp", 0, 0, axis_index_groups=same_parity).astype(f32)

    with jax.named_scope("weight_grad"):
        other_core = [(i, i ^ 1) for i in range(seq_count)]
        other_y = [(i, i ^ 2) for i in range(seq_count)]
        half = jax.ShapeDtypeStruct((width_local // 2, columns), f32)
        by_chunk = student.reshape(8, 2, 64, width_local)
        send, keep = call(
            weight_grad,
            (half, half),
            2 * tokens * width_local * columns,
            5_000_000,
            grid_spec=pltpu.PrefetchScalarGridSpec(
                num_scalar_prefetch=1,
                grid=(4,),
                in_specs=[
                    pl.BlockSpec((8, 1, 64, width_local), lambda i, p: (0, 1 - p[2], 0, 0)),
                    pl.BlockSpec((8, 1, 64, width_local), lambda i, p: (0, p[2], 0, 0)),
                    pl.BlockSpec((tensor_count, own, LANES), lambda i, p: (0, i, 0)),
                    pl.BlockSpec((tensor_count, own, LANES), lambda i, p: (0, i, 0)),
                    pl.BlockSpec((1, META, LANES), lambda i, p: (0, 256 // META, 0)),
                ],
                out_specs=(
                    pl.BlockSpec((width_local // 2, 2 * LANES), lambda i, p: (0, i)),
                    pl.BlockSpec((width_local // 2, 2 * LANES), lambda i, p: (0, i)),
                ),
                scratch_shapes=[pltpu.VMEM((width_local, tokens), bf16)],
            ),
        )(place, by_chunk, by_chunk, grad_a, grad_b, term)
        pair = (keep + lax.ppermute(send, "seq", other_core)).astype(bf16)
        mine = pair.astype(f32) + lax.ppermute(pair, "seq", other_y).astype(f32)
        theirs = lax.ppermute(mine, "seq", other_core)
        grad_weight = jnp.where(
            core == 0,
            jnp.concatenate([mine, theirs], axis=0),
            jnp.concatenate([theirs, mine], axis=0),
        )

    with jax.named_scope("results"):
        grad_input, loss = call(
            finish,
            (jax.ShapeDtypeStruct((own // 2, width_local), bf16), jax.ShapeDtypeStruct((1, LANES), f32)),
            0,
            1_200_000,
            grid=(1,),
            in_specs=[
                pl.BlockSpec((dp_half, chunk, LANES), lambda i: (0, 0, 0)),
                pl.BlockSpec((8, LANES), lambda i: (0, 0)),
            ],
            out_specs=(
                pl.BlockSpec((own // 2, width_local), lambda i: (0, 0)),
                pl.BlockSpec((1, LANES), lambda i: (0, 0)),
            ),
        )(terms, grad_weight)
        grad_input = grad_input.reshape(1, 4, 16, width_local)
        loss_value = loss[0, 0] / (tokens * seq_count * columns * dp_count)
    return (loss_value, grad_weight, grad_input)


def solution(mesh):
    placed = (P("seq", None, None, "tensor"), P("seq", None, "dp", "tensor"), P("tensor", "dp"))
    return jax.shard_map(
        body,
        mesh=mesh,
        in_specs=placed,
        out_specs=(P(), P("tensor", "dp"), P("seq", "dp", None, "tensor")),
        check_vma=False,
    )
```

```python
import jax
import jax.numpy as jnp
from jax import lax
from jax.experimental import pallas as pl
from jax.experimental.pallas import tpu as pltpu
from jax.sharding import PartitionSpec as P

scale_epsilon = 1e-06
grad_factor = 0.25
LANES = 128
META = 8
PIECES = 16
TOP = 14.0
WAITS = 30_000_000_000
bf16, f16, f32 = jnp.bfloat16, jnp.float16, jnp.float32


def call(kernel, out_shape, flops, nbytes, **kw):
    return pl.pallas_call(
        kernel,
        out_shape=out_shape,
        cost_estimate=pl.CostEstimate(flops=flops, bytes_accessed=nbytes, transcendentals=0),
        compiler_params=pltpu.CompilerParams(vmem_limit_bytes=16 * 1024 * 1024),
        **kw,
    )


def all_to_all(x, axis):
    return lax.all_to_all(x, axis, 0, 0)


def butterfly(x, steps):
    for axis, step in steps:
        x = x + lax.ppermute(x, axis, [(i, i ^ step) for i in range(lax.axis_size(axis))])
    return x


def exponent_of(largest):
    return jnp.clip(jnp.ceil(jnp.log2(jnp.maximum(largest, 1e-30))), -100.0, 100.0)


def pack_teacher(place_ref, x_ref, after_ref, *refs):
    del after_ref
    held = refs[4]
    rows = x_ref[...].astype(f32)
    largest = jnp.max(jnp.max(jnp.abs(rows).reshape(8, 8, -1), axis=0), axis=1, keepdims=True)
    wide = jnp.broadcast_to(jnp.concatenate([largest, largest], axis=0), (16, LANES)).astype(bf16)
    half = rows.shape[1] // 4
    for t in range(8):
        for j in range(2):
            block = rows[8 * t : 8 * t + 8, 2 * half * j : 2 * half * (j + 1)]
            both = jnp.concatenate([block[:, :half], block[:, half:]], axis=0)
            low, high = 2 * (t % 2) + j, t // 2
            held[low, 16 * high : 16 * high + 16, :half] = both.astype(bf16)
            held[low, 16 * high : 16 * high + 16, half:] = wide
    for k in range(4):
        refs[k][...] = held[(place_ref[1] + k) & 3]


def regroup_teacher(place_ref, *refs):
    for m in range(4):
        high = (place_ref[0] + m) & 3
        for k in range(4):
            refs[4 + m][16 * k : 16 * k + 16, :] = refs[k][pl.ds(pl.multiple_of(16 * high, 16), 16), :]


def forward(s_ref, w_ref, o_ref, done_ref):
    done_ref[...] = jnp.zeros_like(done_ref)
    partial = jnp.dot(s_ref[...], w_ref[...], preferred_element_type=f32)
    power = exponent_of(jnp.max(jnp.abs(partial), axis=1, keepdims=True))
    scaled = partial * jnp.exp2(TOP - power)
    rows, width = scaled.shape[0] // 2, scaled.shape[1]
    for n in range(2):
        for c in range(width // LANES):
            o_ref[n, c * rows : (c + 1) * rows, :] = scaled[n * rows : (n + 1) * rows, c * LANES : (c + 1) * LANES]
        meta = jnp.transpose(jnp.broadcast_to(power[n * rows : (n + 1) * rows], (rows, LANES)))
        o_ref[n, width // LANES * rows :, :] = meta[:META]


def token_grad(place_ref, pred_ref, t0_ref, t1_ref, t2_ref, t3_ref, a_ref, b_ref, held):
    blocks, rows, _ = pred_ref.shape

    @pl.when(pl.program_id(0) == 0)
    def _():
        arrived = jnp.concatenate([t0_ref[...], t1_ref[...], t2_ref[...], t3_ref[...]], axis=0)
        count, half = arrived.shape[0], blocks // 2 * LANES
        r = lax.broadcasted_iota(jnp.int32, (rows, count), 0)
        q = lax.broadcasted_iota(jnp.int32, (rows, count), 1)
        shift = q // 16 % 4
        shift = jnp.where(shift == 3, -1, shift)
        second = (place_ref[0] * 4 + place_ref[1] - 4 * (q // 64) - shift) & 15
        match = r == (q % 8) * 16 + second
        first = jnp.where(match & (q // 8 % 2 == 0), 1.0, 0.0).astype(bf16)
        other = jnp.where(match & (q // 8 % 2 == 1), 1.0, 0.0).astype(bf16)
        left = jnp.dot(first, arrived, preferred_element_type=f32)
        right = jnp.dot(other, arrived[:, :half], preferred_element_type=f32)
        target = jnp.concatenate([left[:, :half], right], axis=1)
        token_scale = left[:, half : half + 1] + scale_epsilon
        total = jnp.zeros((rows, LANES), f32)
        for c in range(blocks):
            quantized = (target[:, c * LANES : (c + 1) * LANES] / token_scale).astype(bf16)
            difference = pred_ref[c] / token_scale - quantized.astype(f32)
            total = total + difference * difference
            held[c * rows : (c + 1) * rows, :] = ((difference / token_scale) * grad_factor).astype(bf16)
        loss = jnp.sum(jnp.sum(total, axis=0, keepdims=True), axis=1, keepdims=True)
        high = loss.astype(bf16).astype(f32)
        middle = (loss - high).astype(bf16).astype(f32)
        low = loss - high - middle
        row = lax.broadcasted_iota(jnp.int32, (PIECES, LANES), 0)
        pieces = jnp.where(row == 0, high, jnp.where(row == 1, middle, jnp.where(row == 2, low, 0.0)))
        held[blocks * rows :, :] = pieces.astype(bf16)

    part = rows // 2
    for ref, chunk in ((a_ref, 1 - place_ref[2]), (b_ref, place_ref[2])):
        for c in range(blocks):
            start = pl.multiple_of(c * rows + chunk * part, part)
            ref[0, c * part : (c + 1) * part, :] = held[pl.ds(start, part), :]
    a_ref[0, blocks * part :, :] = held[blocks * rows :, :]


def scaled_by_power(chunk):
    largest = jnp.max(jnp.max(jnp.abs(chunk), axis=0, keepdims=True), axis=1, keepdims=True)
    power = exponent_of(largest)
    return chunk * jnp.exp2(TOP - power), power


def loss_rows(loss):
    row = lax.broadcasted_iota(jnp.int32, (META, LANES), 0)
    power = exponent_of(loss)
    scaled = loss * jnp.exp2(10.0 - power)
    high = jnp.floor(scaled)
    rest = (scaled - high) * 2048.0
    middle = jnp.floor(rest)
    low = jnp.floor((rest - middle) * 2048.0)
    return row, jnp.where(row == 1, power, jnp.where(row == 2, high, jnp.where(row == 3, middle, low)))


def chunk_terms(g_ref, w_ref):
    part = 64
    grad = jnp.concatenate(
        [
            jnp.concatenate([g_ref[n, c * part : (c + 1) * part, :] for c in range(8)], axis=1)
            for n in range(g_ref.shape[0])
        ],
        axis=0,
    )
    terms = lax.dot_general(grad, w_ref[...], (((1,), (1,)), ((), ())), preferred_element_type=f32)
    return [terms[n * part : (n + 1) * part] for n in range(g_ref.shape[0])]


def send_terms(g_ref, w_ref, loss_ref, send_ref, total_ref):
    pieces = jnp.sum(loss_ref[...].astype(f32), axis=0)
    total_ref[...] = jnp.sum(pieces, axis=0, keepdims=True)
    for n, chunk in enumerate(chunk_terms(g_ref, w_ref)):
        scaled, power = scaled_by_power(chunk)
        for c in range(4):
            send_ref[n, 64 * c : 64 * c + 64, :] = scaled[:, c * LANES : (c + 1) * LANES]
        send_ref[n, 256:, :] = jnp.broadcast_to(power, (META, LANES))


def keep_terms(g_ref, w_ref, got_ref, loss_ref, o_ref):
    row, meta = loss_rows(loss_ref[...])
    for n, chunk in enumerate(chunk_terms(g_ref, w_ref)):
        got = jnp.concatenate([got_ref[n, 64 * c : 64 * c + 64, :] for c in range(4)], axis=1)
        chunk = chunk + got * jnp.exp2(got_ref[n, 256:257, 0:1] - TOP)
        scaled, power = scaled_by_power(chunk)
        for c in range(4):
            o_ref[n, 64 * c : 64 * c + 64, :] = scaled[:, c * LANES : (c + 1) * LANES]
        o_ref[n, 256:, :] = jnp.where(row == 0, power, meta)


def weight_grad(place_ref, s_ref, t_ref, g_ref, h_ref, after_ref, send_ref, keep_ref, held):
    del after_ref
    width = s_ref.shape[-1]
    half, part = width // 2, 64
    core = place_ref[3]

    @pl.when(pl.program_id(0) == 0)
    def _():
        for n, which in enumerate((1 - core, core)):
            lanes = pl.ds(pl.multiple_of(which * half, half), half)
            student = jnp.concatenate([x[:, 0, :, lanes].reshape(-1, half) for x in (s_ref, t_ref)], axis=0)
            held[n * half : (n + 1) * half, :] = student.T

    def columns(ref):
        parts = [ref[:, c * part : (c + 1) * part, :].reshape(-1, LANES) for c in range(4)]
        return jnp.concatenate(parts, axis=1)

    grad = jnp.concatenate([columns(g_ref), columns(h_ref)], axis=0)
    send_ref[...] = jnp.dot(held[:half, :], grad, preferred_element_type=f32)
    keep_ref[...] = jnp.dot(held[half:, :], grad, preferred_element_type=f32)


def finish(terms_ref, after_ref, o_ref, loss_ref):
    del after_ref
    total = jnp.zeros(terms_ref.shape[1:], f32)[:256]
    loss = jnp.zeros((1, LANES), f32)
    for n in range(terms_ref.shape[0]):
        meta = terms_ref[n, 256:, :]
        total = total + terms_ref[n, :256, :] * jnp.exp2(meta[:1] - TOP)
        loss = loss + (meta[2:3] + (meta[3:4] + meta[4:5] / 2048.0) / 2048.0) * jnp.exp2(meta[1:2] - 10.0)
    loss_ref[...] = loss
    for c in range(4):
        o_ref[:, c * LANES : (c + 1) * LANES] = total[64 * c : 64 * c + 64].astype(bf16)


def body(student_hidden, teacher_hidden, proj_weight):
    width_local = student_hidden.shape[3]
    student = student_hidden.reshape(-1, width_local)
    tokens, columns = student.shape[0], proj_weight.shape[1]
    tensor_count, dp_count, seq_count = (lax.axis_size(a) for a in ("tensor", "dp", "seq"))
    own = tokens // tensor_count
    blocks = columns // LANES

    dp_index = lax.axis_index("dp").astype(jnp.int32)
    core = (lax.axis_index("seq") % 2).astype(jnp.int32)
    place = jnp.stack([dp_index // 4, dp_index % 4, dp_index % 2, core])
    scalars = pl.BlockSpec(memory_space=pltpu.SMEM)
    whole = pl.BlockSpec(memory_space=pltpu.VMEM)

    with jax.named_scope("teacher"):
        spread = all_to_all(teacher_hidden.reshape(8, 8, -1), "tensor")
        size = blocks * own + META
        partial, done = call(
            forward,
            (
                jax.ShapeDtypeStruct((tensor_count, size, LANES), f32),
                jax.ShapeDtypeStruct((META, LANES), f32),
            ),
            2 * tokens * width_local * columns,
            6_000_000,
            grid=(tensor_count // 2,),
            in_specs=[
                pl.BlockSpec((2 * own, width_local), lambda i: (i, 0)),
                pl.BlockSpec((width_local, columns), lambda i: (0, 0)),
            ],
            out_specs=(
                pl.BlockSpec((2, size, LANES), lambda i: (i, 0, 0)),
                pl.BlockSpec((META, LANES), lambda i: (0, 0)),
            ),
        )(student, proj_weight)
        partial, done = lax.optimization_barrier((partial.astype(f16), done))
        group = (jax.ShapeDtypeStruct((64, columns // 2 + LANES), bf16),) * 4
        packed = call(
            pack_teacher,
            group,
            0,
            600_000,
            grid=(1,),
            in_specs=[
                scalars,
                pl.BlockSpec((64, 2 * columns), lambda i: (0, 0)),
                pl.BlockSpec((META, LANES), lambda i: (0, 0)),
            ],
            out_specs=(pl.BlockSpec(group[0].shape, lambda i: (0, 0)),) * 4,
            scratch_shapes=[pltpu.VMEM((4, 64, columns // 2 + LANES), bf16)],
        )(place, spread.reshape(64, -1), done)
        near = [packed[0]]
        for k in range(1, 4):
            moves = [(z, (z + (k if k < 3 else -1)) % dp_count) for z in range(dp_count)]
            near.append(lax.ppermute(packed[k], "dp", moves))
        packed = call(
            regroup_teacher,
            group,
            WAITS,
            600_000,
            in_specs=[scalars] + [whole] * 4,
            out_specs=(whole,) * 4,
        )(place, *near)
        target = [packed[0]]
        for m in range(1, 4):
            moves = [(z, (z + 4 * m) % dp_count) for z in range(dp_count)]
            target.append(lax.ppermute(packed[m], "dp", moves))

    with jax.named_scope("prediction"):
        parts = all_to_all(partial, "tensor").astype(f32)
        unscale = jnp.exp2(parts[:, blocks * own, :] - TOP)
        data = parts[:, : blocks * own, :].reshape(tensor_count, blocks, own, LANES)
        prediction = jnp.sum(data * unscale[:, None, :, None], axis=0)

    with jax.named_scope("gradient"):
        part = blocks * own // 2
        block_a = pl.BlockSpec((1, part + PIECES, LANES), lambda i: (i, 0, 0))
        block_b = pl.BlockSpec((1, part, LANES), lambda i: (i, 0, 0))
        own_a, own_b = call(
            token_grad,
            (
                jax.ShapeDtypeStruct((tensor_count, part + PIECES, LANES), bf16),
                jax.ShapeDtypeStruct((tensor_count, part, LANES), bf16),
            ),
            2 * own * own * columns,
            3_000_000,
            grid=(tensor_count,),
            in_specs=[scalars, pl.BlockSpec((blocks, own, LANES), lambda i: (0, 0, 0))]
            + [pl.BlockSpec(group[0].shape, lambda i: (0, 0))] * 4,
            out_specs=(block_a, block_b),
            scratch_shapes=[pltpu.VMEM((blocks * own + PIECES, LANES), bf16)],
        )(place, prediction, *target)
        grad_a = all_to_all(own_a, "tensor")
        grad_b = all_to_all(own_b, "tensor")

    with jax.named_scope("input_grad"):
        chunk = 64 * 4 + META
        dp_half = dp_count // 2
        half_terms = jax.ShapeDtypeStruct((dp_half, chunk, LANES), f32)
        weights = pl.BlockSpec((width_local, columns), lambda i: (0, 0))
        losses = pl.BlockSpec((1, LANES), lambda i: (0, 0))
        block = pl.BlockSpec((8, chunk, LANES), lambda i: (i, 0, 0))
        send, total = call(
            send_terms,
            (half_terms, jax.ShapeDtypeStruct((1, LANES), f32)),
            tokens * width_local * columns,
            4_000_000,
            grid=(1,),
            in_specs=[
                pl.BlockSpec((8, part + PIECES, LANES), lambda i: (i, 0, 0)),
                weights,
                pl.BlockSpec((tensor_count, PIECES, LANES), lambda i: (0, part // PIECES, 0)),
            ],
            out_specs=(block, losses),
        )(grad_a, proj_weight, grad_a)
        neighbour = [(z, z ^ 1) for z in range(dp_count)]
        loss = butterfly(total, (("seq", 1), ("seq", 2), ("dp", 1)))
        got = lax.ppermute(send.astype(f16), "dp", neighbour)
        got = lax.optimization_barrier((got, grad_b))[0].astype(f32)
        term = call(
            keep_terms,
            half_terms,
            tokens * width_local * columns,
            5_000_000,
            grid=(1,),
            in_specs=[pl.BlockSpec((8, part, LANES), lambda i: (i, 0, 0)), weights, block, losses],
            out_specs=block,
        )(grad_b, proj_weight, got, loss)
        same_parity = [list(range(p, dp_count, 2)) for p in range(2)]
        terms = lax.all_to_all(term.astype(f16), "dp", 0, 0, axis_index_groups=same_parity).astype(f32)

    with jax.named_scope("weight_grad"):
        other_core = [(i, i ^ 1) for i in range(seq_count)]
        other_y = [(i, i ^ 2) for i in range(seq_count)]
        half = jax.ShapeDtypeStruct((width_local // 2, columns), f32)
        by_chunk = student.reshape(8, 2, 64, width_local)
        send, keep = call(
            weight_grad,
            (half, half),
            2 * tokens * width_local * columns,
            5_000_000,
            grid_spec=pltpu.PrefetchScalarGridSpec(
                num_scalar_prefetch=1,
                grid=(2,),
                in_specs=[
                    pl.BlockSpec((8, 1, 64, width_local), lambda i, p: (0, 1 - p[2], 0, 0)),
                    pl.BlockSpec((8, 1, 64, width_local), lambda i, p: (0, p[2], 0, 0)),
                    pl.BlockSpec((tensor_count, 2 * own, LANES), lambda i, p: (0, i, 0)),
                    pl.BlockSpec((tensor_count, 2 * own, LANES), lambda i, p: (0, i, 0)),
                    pl.BlockSpec((1, META, LANES), lambda i, p: (0, 256 // META, 0)),
                ],
                out_specs=(
                    pl.BlockSpec((width_local // 2, 4 * LANES), lambda i, p: (0, i)),
                    pl.BlockSpec((width_local // 2, 4 * LANES), lambda i, p: (0, i)),
                ),
                scratch_shapes=[pltpu.VMEM((width_local, tokens), bf16)],
            ),
        )(place, by_chunk, by_chunk, grad_a, grad_b, term)
        pair = (keep + lax.ppermute(send, "seq", other_core)).astype(bf16)
        mine = pair.astype(f32) + lax.ppermute(pair, "seq", other_y).astype(f32)
        theirs = lax.ppermute(mine, "seq", other_core)
        grad_weight = jnp.where(
            core == 0,
            jnp.concatenate([mine, theirs], axis=0),
            jnp.concatenate([theirs, mine], axis=0),
        )

    with jax.named_scope("results"):
        grad_input, loss = call(
            finish,
            (jax.ShapeDtypeStruct((own // 2, width_local), bf16), jax.ShapeDtypeStruct((1, LANES), f32)),
            0,
            1_200_000,
            grid=(1,),
            in_specs=[
                pl.BlockSpec((dp_half, chunk, LANES), lambda i: (0, 0, 0)),
                pl.BlockSpec((8, LANES), lambda i: (0, 0)),
            ],
            out_specs=(
                pl.BlockSpec((own // 2, width_local), lambda i: (0, 0)),
                pl.BlockSpec((1, LANES), lambda i: (0, 0)),
            ),
        )(terms, grad_weight)
        grad_input = grad_input.reshape(1, 4, 16, width_local)
        loss_value = loss[0, 0] / (tokens * seq_count * columns * dp_count)
    return (loss_value, grad_weight, grad_input)


def solution(mesh):
    placed = (P("seq", None, None, "tensor"), P("seq", None, "dp", "tensor"), P("tensor", "dp"))
    return jax.shard_map(
        body,
        mesh=mesh,
        in_specs=placed,
        out_specs=(P(), P("tensor", "dp"), P("seq", "dp", None, "tensor")),
        check_vma=False,
    )
```

```python
import jax
import jax.numpy as jnp
from jax import lax
from jax.experimental import pallas as pl
from jax.experimental.pallas import tpu as pltpu
from jax.sharding import PartitionSpec as P

scale_epsilon = 1e-06
grad_factor = 0.25
LANES = 128
META = 8
PIECES = 16
TOP = 14.0
WAITS = 30_000_000_000
bf16, f16, f32 = jnp.bfloat16, jnp.float16, jnp.float32


def call(kernel, out_shape, flops, nbytes, **kw):
    return pl.pallas_call(
        kernel,
        out_shape=out_shape,
        cost_estimate=pl.CostEstimate(flops=flops, bytes_accessed=nbytes, transcendentals=0),
        compiler_params=pltpu.CompilerParams(vmem_limit_bytes=16 * 1024 * 1024),
        **kw,
    )


def all_to_all(x, axis):
    return lax.all_to_all(x, axis, 0, 0)


def butterfly(x, steps):
    for axis, step in steps:
        x = x + lax.ppermute(x, axis, [(i, i ^ step) for i in range(lax.axis_size(axis))])
    return x


def exponent_of(largest):
    return jnp.clip(jnp.ceil(jnp.log2(jnp.maximum(largest, 1e-30))), -100.0, 100.0)


def pack_teacher(place_ref, x_ref, after_ref, *refs):
    del after_ref
    held = refs[4]
    rows = x_ref[...].astype(f32)
    largest = jnp.max(jnp.max(jnp.abs(rows).reshape(8, 8, -1), axis=0), axis=1, keepdims=True)
    wide = jnp.broadcast_to(jnp.concatenate([largest, largest], axis=0), (16, LANES)).astype(bf16)
    half = rows.shape[1] // 4
    for t in range(8):
        for j in range(2):
            block = rows[8 * t : 8 * t + 8, 2 * half * j : 2 * half * (j + 1)]
            both = jnp.concatenate([block[:, :half], block[:, half:]], axis=0)
            low, high = 2 * (t % 2) + j, t // 2
            held[low, 16 * high : 16 * high + 16, :half] = both.astype(bf16)
            held[low, 16 * high : 16 * high + 16, half:] = wide
    for k in range(4):
        refs[k][...] = held[(place_ref[1] + k) & 3]


def regroup_teacher(place_ref, *refs):
    for m in range(4):
        high = (place_ref[0] + m) & 3
        for k in range(4):
            refs[4 + m][16 * k : 16 * k + 16, :] = refs[k][pl.ds(pl.multiple_of(16 * high, 16), 16), :]


def forward(s_ref, w_ref, o_ref, done_ref):
    done_ref[...] = jnp.zeros_like(done_ref)
    partial = jnp.dot(s_ref[...], w_ref[...], preferred_element_type=f32)
    power = exponent_of(jnp.max(jnp.abs(partial), axis=1, keepdims=True))
    scaled = partial * jnp.exp2(TOP - power)
    rows, width = scaled.shape[0] // 4, scaled.shape[1]
    for n in range(4):
        for c in range(width // LANES):
            o_ref[n, c * rows : (c + 1) * rows, :] = scaled[n * rows : (n + 1) * rows, c * LANES : (c + 1) * LANES]
        meta = jnp.transpose(jnp.broadcast_to(power[n * rows : (n + 1) * rows], (rows, LANES)))
        o_ref[n, width // LANES * rows :, :] = meta[:META]


def token_grad(place_ref, pred_ref, t0_ref, t1_ref, t2_ref, t3_ref, a_ref, b_ref, held):
    blocks, rows, _ = pred_ref.shape

    @pl.when(pl.program_id(0) == 0)
    def _():
        arrived = jnp.concatenate([t0_ref[...], t1_ref[...], t2_ref[...], t3_ref[...]], axis=0)
        count, half = arrived.shape[0], blocks // 2 * LANES
        r = lax.broadcasted_iota(jnp.int32, (rows, count), 0)
        q = lax.broadcasted_iota(jnp.int32, (rows, count), 1)
        shift = q // 16 % 4
        shift = jnp.where(shift == 3, -1, shift)
        second = (place_ref[0] * 4 + place_ref[1] - 4 * (q // 64) - shift) & 15
        match = r == (q % 8) * 16 + second
        first = jnp.where(match & (q // 8 % 2 == 0), 1.0, 0.0).astype(bf16)
        other = jnp.where(match & (q // 8 % 2 == 1), 1.0, 0.0).astype(bf16)
        left = jnp.dot(first, arrived, preferred_element_type=f32)
        right = jnp.dot(other, arrived[:, :half], preferred_element_type=f32)
        target = jnp.concatenate([left[:, :half], right], axis=1)
        token_scale = left[:, half : half + 1] + scale_epsilon
        total = jnp.zeros((rows, LANES), f32)
        for c in range(blocks):
            quantized = (target[:, c * LANES : (c + 1) * LANES] / token_scale).astype(bf16)
            difference = pred_ref[c] / token_scale - quantized.astype(f32)
            total = total + difference * difference
            held[c * rows : (c + 1) * rows, :] = ((difference / token_scale) * grad_factor).astype(bf16)
        loss = jnp.sum(jnp.sum(total, axis=0, keepdims=True), axis=1, keepdims=True)
        high = loss.astype(bf16).astype(f32)
        middle = (loss - high).astype(bf16).astype(f32)
        low = loss - high - middle
        row = lax.broadcasted_iota(jnp.int32, (PIECES, LANES), 0)
        pieces = jnp.where(row == 0, high, jnp.where(row == 1, middle, jnp.where(row == 2, low, 0.0)))
        held[blocks * rows :, :] = pieces.astype(bf16)

    part = rows // 2
    for ref, chunk in ((a_ref, 1 - place_ref[2]), (b_ref, place_ref[2])):
        for c in range(blocks):
            start = pl.multiple_of(c * rows + chunk * part, part)
            ref[0, c * part : (c + 1) * part, :] = held[pl.ds(start, part), :]
    a_ref[0, blocks * part :, :] = held[blocks * rows :, :]


def scaled_by_power(chunk):
    largest = jnp.max(jnp.max(jnp.abs(chunk), axis=0, keepdims=True), axis=1, keepdims=True)
    power = exponent_of(largest)
    return chunk * jnp.exp2(TOP - power), power


def loss_rows(loss):
    row = lax.broadcasted_iota(jnp.int32, (META, LANES), 0)
    power = exponent_of(loss)
    scaled = loss * jnp.exp2(10.0 - power)
    high = jnp.floor(scaled)
    rest = (scaled - high) * 2048.0
    middle = jnp.floor(rest)
    low = jnp.floor((rest - middle) * 2048.0)
    return row, jnp.where(row == 1, power, jnp.where(row == 2, high, jnp.where(row == 3, middle, low)))


def chunk_terms(g_ref, w_ref):
    part = 64
    grad = jnp.concatenate(
        [
            jnp.concatenate([g_ref[n, c * part : (c + 1) * part, :] for c in range(8)], axis=1)
            for n in range(g_ref.shape[0])
        ],
        axis=0,
    )
    terms = lax.dot_general(grad, w_ref[...], (((1,), (1,)), ((), ())), preferred_element_type=f32)
    return [terms[n * part : (n + 1) * part] for n in range(g_ref.shape[0])]


def send_terms(g_ref, w_ref, loss_ref, send_ref, total_ref):
    pieces = jnp.sum(loss_ref[...].astype(f32), axis=0)
    total_ref[...] = jnp.sum(pieces, axis=0, keepdims=True)
    for n, chunk in enumerate(chunk_terms(g_ref, w_ref)):
        scaled, power = scaled_by_power(chunk)
        for c in range(4):
            send_ref[n, 64 * c : 64 * c + 64, :] = scaled[:, c * LANES : (c + 1) * LANES]
        send_ref[n, 256:, :] = jnp.broadcast_to(power, (META, LANES))


def keep_terms(g_ref, w_ref, got_ref, loss_ref, o_ref):
    row, meta = loss_rows(loss_ref[...])
    for n, chunk in enumerate(chunk_terms(g_ref, w_ref)):
        got = jnp.concatenate([got_ref[n, 64 * c : 64 * c + 64, :] for c in range(4)], axis=1)
        chunk = chunk + got * jnp.exp2(got_ref[n, 256:257, 0:1] - TOP)
        scaled, power = scaled_by_power(chunk)
        for c in range(4):
            o_ref[n, 64 * c : 64 * c + 64, :] = scaled[:, c * LANES : (c + 1) * LANES]
        o_ref[n, 256:, :] = jnp.where(row == 0, power, meta)


def weight_grad(place_ref, s_ref, t_ref, g_ref, h_ref, after_ref, send_ref, keep_ref, held):
    del after_ref
    width = s_ref.shape[-1]
    half, part = width // 2, 64
    core = place_ref[3]

    @pl.when(pl.program_id(0) == 0)
    def _():
        for n, which in enumerate((1 - core, core)):
            lanes = pl.ds(pl.multiple_of(which * half, half), half)
            student = jnp.concatenate([x[:, 0, :, lanes].reshape(-1, half) for x in (s_ref, t_ref)], axis=0)
            held[n * half : (n + 1) * half, :] = student.T

    def columns(ref):
        parts = [ref[:, c * part : (c + 1) * part, :].reshape(-1, LANES) for c in range(8)]
        return jnp.concatenate(parts, axis=1)

    grad = jnp.concatenate([columns(g_ref), columns(h_ref)], axis=0)
    send_ref[...] = jnp.dot(held[:half, :], grad, preferred_element_type=f32)
    keep_ref[...] = jnp.dot(held[half:, :], grad, preferred_element_type=f32)


def finish(terms_ref, after_ref, o_ref, loss_ref):
    del after_ref
    total = jnp.zeros(terms_ref.shape[1:], f32)[:256]
    loss = jnp.zeros((1, LANES), f32)
    for n in range(terms_ref.shape[0]):
        meta = terms_ref[n, 256:, :]
        total = total + terms_ref[n, :256, :] * jnp.exp2(meta[:1] - TOP)
        loss = loss + (meta[2:3] + (meta[3:4] + meta[4:5] / 2048.0) / 2048.0) * jnp.exp2(meta[1:2] - 10.0)
    loss_ref[...] = loss
    for c in range(4):
        o_ref[:, c * LANES : (c + 1) * LANES] = total[64 * c : 64 * c + 64].astype(bf16)


def body(student_hidden, teacher_hidden, proj_weight):
    width_local = student_hidden.shape[3]
    student = student_hidden.reshape(-1, width_local)
    tokens, columns = student.shape[0], proj_weight.shape[1]
    tensor_count, dp_count, seq_count = (lax.axis_size(a) for a in ("tensor", "dp", "seq"))
    own = tokens // tensor_count
    blocks = columns // LANES

    dp_index = lax.axis_index("dp").astype(jnp.int32)
    core = (lax.axis_index("seq") % 2).astype(jnp.int32)
    place = jnp.stack([dp_index // 4, dp_index % 4, dp_index % 2, core])
    scalars = pl.BlockSpec(memory_space=pltpu.SMEM)
    whole = pl.BlockSpec(memory_space=pltpu.VMEM)

    with jax.named_scope("teacher"):
        spread = all_to_all(teacher_hidden.reshape(8, 8, -1), "tensor")
        size = blocks * own + META
        partial, done = call(
            forward,
            (
                jax.ShapeDtypeStruct((tensor_count, size, LANES), f32),
                jax.ShapeDtypeStruct((META, LANES), f32),
            ),
            2 * tokens * width_local * columns,
            6_000_000,
            grid=(tensor_count // 4,),
            in_specs=[
                pl.BlockSpec((4 * own, width_local), lambda i: (i, 0)),
                pl.BlockSpec((width_local, columns), lambda i: (0, 0)),
            ],
            out_specs=(
                pl.BlockSpec((4, size, LANES), lambda i: (i, 0, 0)),
                pl.BlockSpec((META, LANES), lambda i: (0, 0)),
            ),
        )(student, proj_weight)
        partial, done = lax.optimization_barrier((partial.astype(f16), done))
        group = (jax.ShapeDtypeStruct((64, columns // 2 + LANES), bf16),) * 4
        packed = call(
            pack_teacher,
            group,
            0,
            600_000,
            grid=(1,),
            in_specs=[
                scalars,
                pl.BlockSpec((64, 2 * columns), lambda i: (0, 0)),
                pl.BlockSpec((META, LANES), lambda i: (0, 0)),
            ],
            out_specs=(pl.BlockSpec(group[0].shape, lambda i: (0, 0)),) * 4,
            scratch_shapes=[pltpu.VMEM((4, 64, columns // 2 + LANES), bf16)],
        )(place, spread.reshape(64, -1), done)
        near = [packed[0]]
        for k in range(1, 4):
            moves = [(z, (z + (k if k < 3 else -1)) % dp_count) for z in range(dp_count)]
            near.append(lax.ppermute(packed[k], "dp", moves))
        packed = call(
            regroup_teacher,
            group,
            WAITS,
            600_000,
            in_specs=[scalars] + [whole] * 4,
            out_specs=(whole,) * 4,
        )(place, *near)
        target = [packed[0]]
        for m in range(1, 4):
            moves = [(z, (z + 4 * m) % dp_count) for z in range(dp_count)]
            target.append(lax.ppermute(packed[m], "dp", moves))

    with jax.named_scope("prediction"):
        parts = all_to_all(partial, "tensor").astype(f32)
        unscale = jnp.exp2(parts[:, blocks * own, :] - TOP)
        data = parts[:, : blocks * own, :].reshape(tensor_count, blocks, own, LANES)
        prediction = jnp.sum(data * unscale[:, None, :, None], axis=0)

    with jax.named_scope("gradient"):
        part = blocks * own // 2
        block_a = pl.BlockSpec((1, part + PIECES, LANES), lambda i: (i, 0, 0))
        block_b = pl.BlockSpec((1, part, LANES), lambda i: (i, 0, 0))
        own_a, own_b = call(
            token_grad,
            (
                jax.ShapeDtypeStruct((tensor_count, part + PIECES, LANES), bf16),
                jax.ShapeDtypeStruct((tensor_count, part, LANES), bf16),
            ),
            2 * own * own * columns,
            3_000_000,
            grid=(tensor_count,),
            in_specs=[scalars, pl.BlockSpec((blocks, own, LANES), lambda i: (0, 0, 0))]
            + [pl.BlockSpec(group[0].shape, lambda i: (0, 0))] * 4,
            out_specs=(block_a, block_b),
            scratch_shapes=[pltpu.VMEM((blocks * own + PIECES, LANES), bf16)],
        )(place, prediction, *target)
        grad_a = all_to_all(own_a, "tensor")
        grad_b = all_to_all(own_b, "tensor")

    with jax.named_scope("input_grad"):
        chunk = 64 * 4 + META
        dp_half = dp_count // 2
        half_terms = jax.ShapeDtypeStruct((dp_half, chunk, LANES), f32)
        weights = pl.BlockSpec((width_local, columns), lambda i: (0, 0))
        losses = pl.BlockSpec((1, LANES), lambda i: (0, 0))
        block = pl.BlockSpec((8, chunk, LANES), lambda i: (i, 0, 0))
        send, total = call(
            send_terms,
            (half_terms, jax.ShapeDtypeStruct((1, LANES), f32)),
            tokens * width_local * columns,
            4_000_000,
            grid=(1,),
            in_specs=[
                pl.BlockSpec((8, part + PIECES, LANES), lambda i: (i, 0, 0)),
                weights,
                pl.BlockSpec((tensor_count, PIECES, LANES), lambda i: (0, part // PIECES, 0)),
            ],
            out_specs=(block, losses),
        )(grad_a, proj_weight, grad_a)
        neighbour = [(z, z ^ 1) for z in range(dp_count)]
        loss = butterfly(total, (("seq", 1), ("seq", 2), ("dp", 1)))
        got = lax.ppermute(send.astype(f16), "dp", neighbour)
        got = lax.optimization_barrier((got, grad_b))[0].astype(f32)
        term = call(
            keep_terms,
            half_terms,
            tokens * width_local * columns,
            5_000_000,
            grid=(1,),
            in_specs=[pl.BlockSpec((8, part, LANES), lambda i: (i, 0, 0)), weights, block, losses],
            out_specs=block,
        )(grad_b, proj_weight, got, loss)
        same_parity = [list(range(p, dp_count, 2)) for p in range(2)]
        terms = lax.all_to_all(term.astype(f16), "dp", 0, 0, axis_index_groups=same_parity).astype(f32)

    with jax.named_scope("weight_grad"):
        other_core = [(i, i ^ 1) for i in range(seq_count)]
        other_y = [(i, i ^ 2) for i in range(seq_count)]
        half = jax.ShapeDtypeStruct((width_local // 2, columns), f32)
        by_chunk = student.reshape(8, 2, 64, width_local)
        send, keep = call(
            weight_grad,
            (half, half),
            2 * tokens * width_local * columns,
            5_000_000,
            grid_spec=pltpu.PrefetchScalarGridSpec(
                num_scalar_prefetch=1,
                grid=(1,),
                in_specs=[
                    pl.BlockSpec((8, 1, 64, width_local), lambda i, p: (0, 1 - p[2], 0, 0)),
                    pl.BlockSpec((8, 1, 64, width_local), lambda i, p: (0, p[2], 0, 0)),
                    pl.BlockSpec((tensor_count, 4 * own, LANES), lambda i, p: (0, i, 0)),
                    pl.BlockSpec((tensor_count, 4 * own, LANES), lambda i, p: (0, i, 0)),
                    pl.BlockSpec((1, META, LANES), lambda i, p: (0, 256 // META, 0)),
                ],
                out_specs=(
                    pl.BlockSpec((width_local // 2, 8 * LANES), lambda i, p: (0, i)),
                    pl.BlockSpec((width_local // 2, 8 * LANES), lambda i, p: (0, i)),
                ),
                scratch_shapes=[pltpu.VMEM((width_local, tokens), bf16)],
            ),
        )(place, by_chunk, by_chunk, grad_a, grad_b, term)
        pair = (keep + lax.ppermute(send, "seq", other_core)).astype(bf16)
        mine = pair.astype(f32) + lax.ppermute(pair, "seq", other_y).astype(f32)
        theirs = lax.ppermute(mine, "seq", other_core)
        grad_weight = jnp.where(
            core == 0,
            jnp.concatenate([mine, theirs], axis=0),
            jnp.concatenate([theirs, mine], axis=0),
        )

    with jax.named_scope("results"):
        grad_input, loss = call(
            finish,
            (jax.ShapeDtypeStruct((own // 2, width_local), bf16), jax.ShapeDtypeStruct((1, LANES), f32)),
            0,
            1_200_000,
            grid=(1,),
            in_specs=[
                pl.BlockSpec((dp_half, chunk, LANES), lambda i: (0, 0, 0)),
                pl.BlockSpec((8, LANES), lambda i: (0, 0)),
            ],
            out_specs=(
                pl.BlockSpec((own // 2, width_local), lambda i: (0, 0)),
                pl.BlockSpec((1, LANES), lambda i: (0, 0)),
            ),
        )(terms, grad_weight)
        grad_input = grad_input.reshape(1, 4, 16, width_local)
        loss_value = loss[0, 0] / (tokens * seq_count * columns * dp_count)
    return (loss_value, grad_weight, grad_input)


def solution(mesh):
    placed = (P("seq", None, None, "tensor"), P("seq", None, "dp", "tensor"), P("tensor", "dp"))
    return jax.shard_map(
        body,
        mesh=mesh,
        in_specs=placed,
        out_specs=(P(), P("tensor", "dp"), P("seq", "dp", None, "tensor")),
        check_vma=False,
    )
```
